32 devices in a mesh: seq: 8 (over z, x), head: 4 (over y, core).
Axes of the slice: x: 2, y: 2, z: 4, core: 2. Of those that a mesh axis runs over, the one named last changes fastest.
Arguments:
- queries: bfloat16 [4096, 4096], P('seq', 'head'), may hold values from -24 to 24
- key_states: bfloat16 [4096, 4096], P('seq', 'head'), may hold values from -24 to 24
- value_states: bfloat16 [4096, 4096], P('seq', 'head'), may hold values from -6 to 6
- forward_out: bfloat16 [4096, 4096], P('seq', 'head'), may hold values from -3 to 3
- grad_out: bfloat16 [4096, 4096], P('seq', 'head'), may hold values from -96 to 96
- random_blocks: int32 [64, 32, 3], P(None, 'head'), may hold values from 0 to 63, as said below
- global_blocks: int32 [2], replicated, may hold values from 0 to 63, as said below
Outputs:
- grad_queries: bfloat16 [4096, 4096], P(('seq', 'head'))
- grad_keys: bfloat16 [4096, 4096], P(('seq', 'head'))
- grad_values: bfloat16 [4096, 4096], P(('seq', 'head'))
The draws below stay inside these ranges and needn't reach their ends.
Inputs may be any that keep to these rules, and one draw needn't show every extreme that they name: `random_blocks`: for the query blocks of one shard of 512 tokens and the 8 heads of one head group, at most 30 of the 192 entries name blocks held by any one shard of 8 blocks, and one shard, the same for every group, is named exactly 30 times by every group. `global_blocks`: two different blocks, one of them the last block 63.
All inputs are finite; a program needn't handle non-finite values.
Results may differ from the reference program's by a relative error of at most 0.0053.
Values may be sent and summed in bfloat16 or wider, within the bound.
No kernel may reach another device: no remote copies, remote signals or barrier semaphores. Data moves between devices by JAX's collectives and lax.ppermute only.
A program may use at most 128 MiB of HBM per device.

```python
import jax
import jax.numpy as jnp
from jax import lax

HEADS = 32
DH = 128
BS = 64
HD = 8
QB_DEV = 8
NB = 64
SEQ = 4096
REQUESTS = 192
SLOTS = 30


def draw_pair(key):
    base = jax.random.fold_in(key, 7)
    key_query, key_keys = jax.random.split(base, 2)
    shape = (SEQ, HEADS * DH)
    query_draw = jax.random.truncated_normal(key_query, -6.0, 6.0, shape, jnp.float32)
    keys_draw = jax.random.truncated_normal(key_keys, -6.0, 6.0, shape, jnp.float32)
    return (query_draw, keys_draw)


def draw_queries(key, part):
    return draw_pair(key)[0].astype(jnp.bfloat16)


def draw_key_states(key, part):
    return draw_pair(key)[1].astype(jnp.bfloat16)


def draw_random_blocks(key, part):
    seq_count = NB // QB_DEV
    group_count = HEADS // HD
    key_hot, key_groups = jax.random.split(jax.random.fold_in(key, 11))
    hot_owner = jax.random.randint(key_hot, (), 0, seq_count)

    def one_group(group_key):
        key_pool, key_order, key_local = jax.random.split(group_key, 3)
        others = jnp.arange(seq_count - 1, dtype=jnp.int32)
        others = others + (others >= hot_owner).astype(jnp.int32)
        pool = jnp.repeat(others, SLOTS, total_repeat_length=(seq_count - 1) * SLOTS)
        pool = jax.random.permutation(key_pool, pool)[:REQUESTS - SLOTS]
        owners = jnp.concatenate([jnp.full((SLOTS,), hot_owner, jnp.int32), pool])
        owners = jax.random.permutation(key_order, owners)
        local_block = jax.random.randint(key_local, (REQUESTS,), 0, QB_DEV)
        return (owners * QB_DEV + local_block).astype(jnp.int32)
    group_keys = jax.random.split(key_groups, seq_count * group_count)
    table = jax.vmap(one_group)(group_keys)
    table = table.reshape(seq_count, group_count, QB_DEV, HD, 3).transpose(0, 2, 1, 3, 4)
    return table.reshape(NB, HEADS, 3)


def draw_global_blocks(key, part):
    key_other, key_flip = jax.random.split(jax.random.fold_in(key, 13))
    other_block = jax.random.randint(key_other, (), 0, NB - 1).astype(jnp.int32)
    last_block = jnp.full((), NB - 1, jnp.int32)
    flip = jax.random.randint(key_flip, (), 0, 2)
    first = jnp.where(flip == 0, other_block, last_block)
    second = jnp.where(flip == 0, last_block, other_block)
    return jnp.stack([first, second]).astype(jnp.int32)


def block_scale(own_key, extent, shards, low, largest):
    gain, own = 1.0, jax.random.fold_in(own_key, 6)
    for position, shards_of in shards:
        heights = jnp.exp(jax.random.uniform(jax.random.fold_in(own, position), (shards_of,), jnp.float32, low / len(shards), largest / len(shards)))
        gain = gain * jnp.repeat(heights, extent[position] // shards_of).reshape([-1 if axis == position else 1 for axis in range(len(extent))])
    return gain


def bell_draw(rng, shape, width, bound, pieces=(), held_as=jnp.bfloat16):
    loudness = block_scale(rng, shape, pieces, -0.22, 0.18) if pieces else 1.0
    entries = jax.random.normal(rng, shape, jnp.float32) * width * loudness
    return jnp.minimum(jnp.maximum(entries, -bound), bound).astype(held_as)


def setup_inputs(seed: int = 0) -> dict:
    arg_keys = jax.random.split(jax.random.key(seed), 8)
    return {
        "queries": draw_queries(jax.random.fold_in(arg_keys[7], 71), 0),
        "key_states": draw_key_states(jax.random.fold_in(arg_keys[7], 71), 0),
        "value_states": bell_draw(arg_keys[2], (SEQ, HEADS * DH), 1.0, 6.0, ((0, 8), (1, 4))),
        "forward_out": bell_draw(arg_keys[3], (SEQ, HEADS * DH), 0.5, 3.0, ((0, 8), (1, 4))),
        "grad_out": bell_draw(arg_keys[4], (SEQ, HEADS * DH), 16.0, 96.0, ((0, 8), (1, 4))),
        "random_blocks": draw_random_blocks(jax.random.fold_in(arg_keys[7], 71), 0),
        "global_blocks": draw_global_blocks(jax.random.fold_in(arg_keys[7], 71), 0),
    }


def round_trip(values):
    return lax.optimization_barrier(values.astype(jnp.bfloat16)).astype(jnp.float32)


def split_heads(array):
    return array.reshape(-1, BS, HEADS, DH).transpose(2, 0, 1, 3)


def merge_heads(array):
    return array.transpose(1, 2, 0, 3).reshape(-1, HEADS * DH)


def head_grads(operands, global_blocks):
    query_row_block, key_rows, value_rows, saved_rows, gradient_row_block, chosen = operands
    block_count = query_row_block.shape[0]
    softmax_scale = DH ** -0.5
    zero_block = jnp.zeros_like(key_rows[:1])

    def listed(rows):
        padded = jnp.concatenate([zero_block, rows, zero_block], axis=0)
        window_set = jnp.stack([padded[:-2], padded[1:-1], padded[2:]], axis=1)
        random_set = rows[chosen]
        global_set = jnp.broadcast_to(rows[global_blocks][None], (block_count, 2, BS, DH))
        return jnp.concatenate([window_set, random_set, global_set], axis=1).astype(jnp.float32)

    gathered_key_block = listed(key_rows)
    gathered_value_block = listed(value_rows)
    block_ids = jnp.arange(block_count)
    always = jnp.ones((block_count,), bool)
    usable = jnp.stack([block_ids > 0, always, block_ids < block_count - 1, always, always, always, always, always], axis=1)
    query_float32 = query_row_block.astype(jnp.float32)
    gradient_float32 = gradient_row_block.astype(jnp.float32)
    logit_scores = softmax_scale * jnp.einsum("zxp,zufp->zxuf", query_float32, gathered_key_block)
    logit_scores = jnp.where(usable[:, None, :, None], logit_scores, -jnp.inf)
    peak_score = jnp.max(logit_scores, axis=(2, 3))
    row_sum = jnp.sum(jnp.exp(logit_scores - peak_score[:, :, None, None]), axis=(2, 3))
    log_norm = peak_score + jnp.log(row_sum)
    weights = jnp.exp(logit_scores - log_norm[:, :, None, None])
    row_dot = jnp.sum(gradient_float32 * saved_rows.astype(jnp.float32), axis=-1)
    weight_gradient = jnp.einsum("zxp,zufp->zxuf", gradient_float32, gathered_value_block)
    dscores = weights * (weight_gradient - row_dot[:, :, None, None])
    weight_lowp = round_trip(weights)
    score_gradient_lowp = round_trip(dscores)
    dq_terms = softmax_scale * jnp.einsum("bqjk,bjkd->bqjd", score_gradient_lowp, gathered_key_block)
    key_gradient_parts = softmax_scale * jnp.einsum("rmnf,rmc->rnfc", score_gradient_lowp, query_float32)
    value_gradient_parts = jnp.einsum("rmnf,rmc->rnfc", weight_lowp, gradient_float32)
    grad_query = jnp.sum(dq_terms[:, :, :3], axis=2) + jnp.sum(dq_terms[:, :, 6:], axis=2)
    grad_query = grad_query + jnp.sum(round_trip(dq_terms[:, :, 3:6]), axis=2)

    def key_side(slot_terms):
        zero_term = jnp.zeros_like(slot_terms[:1, 0])
        gathered = slot_terms[:, 1] + jnp.concatenate([slot_terms[1:, 0], zero_term], axis=0)
        gathered = gathered + jnp.concatenate([zero_term, slot_terms[:-1, 2]], axis=0)
        gathered = gathered.at[chosen.reshape(-1)].add(round_trip(slot_terms[:, 3:6]).reshape(-1, BS, DH))
        gathered = gathered.at[global_blocks].add(jnp.sum(slot_terms[:, 6:], axis=0))
        return gathered.astype(jnp.bfloat16)

    return grad_query.astype(jnp.bfloat16), key_side(key_gradient_parts), key_side(value_gradient_parts)


def reference(queries, key_states, value_states, forward_out, grad_out, random_blocks, global_blocks):
    operands = (split_heads(queries), split_heads(key_states), split_heads(value_states),
                split_heads(forward_out), split_heads(grad_out), random_blocks.transpose(1, 0, 2))
    grad_q, grad_k, grad_v = lax.map(lambda inputs: head_grads(inputs, global_blocks), operands)
    return merge_heads(grad_q), merge_heads(grad_k), merge_heads(grad_v)
```

```python
from functools import partial
import math

import jax
import jax.numpy as jnp
from jax import lax
from jax.experimental import pallas as pl
from jax.experimental.pallas import tpu as pltpu
from jax.sharding import PartitionSpec as P

DH = 128
BS = 64
GROUP = 4
BATCH = 8
LOG2E = math.log2(math.e)
SCALE = DH**-0.5
OFF = 1e30
NT = (((1,), (1,)), ((), ()))
TN = (((0,), (0,)), ((), ()))


def dot(a, b, dims=(((1,), (0,)), ((), ()))):
    return lax.dot_general(a, b, dims, preferred_element_type=jnp.float32)


def aligned(start):
    return pl.multiple_of(start, BS)


def place_group(me, key_refs, key_rows, tokens):
    for j, ref in enumerate(key_refs):
        start = aligned(BS + (lax.rem(me, GROUP) ^ j) * tokens)
        key_rows[pl.ds(start, tokens), :] = ref[...]


def zero_ends(key_rows):
    edge = jnp.zeros((BS, DH), key_rows.dtype)
    key_rows[pl.ds(0, BS), :] = edge
    key_rows[pl.ds(key_rows.shape[0] - BS, BS), :] = edge


def local_block(block, group, group_blocks):
    place = block - group * group_blocks
    inside = (place >= 0) & (place < group_blocks)
    return jnp.where(inside, place, 0), inside


def edge_block(src, b, blocks, seq_count, group, group_blocks):
    last = blocks - 1
    if b == 0:
        return local_block(src * blocks - 1, group, group_blocks)
    if b == last:
        return local_block((src + 1) * blocks, group, group_blocks)
    return None


def norm_kernel(sizes, meta, table, *refs):
    seq_count, remote, blocks, heads = sizes
    sources = remote + 1
    tokens = blocks * BS
    q_refs = refs[:sources]
    k_refs = refs[sources : sources + GROUP]
    out_ref, key_rows = refs[sources + GROUP :]
    head = pl.program_id(0)
    me = meta[0]
    group = me // GROUP
    group_blocks = GROUP * blocks
    c2 = SCALE * LOG2E

    @pl.when(head == 0)
    def _():
        zero_ends(key_rows)

    place_group(me, k_refs, key_rows, tokens)
    globs = [local_block(meta[1 + j], group, group_blocks) for j in range(2)]
    glob_keys = [key_rows[pl.ds(aligned(BS + p * BS), BS), :] for p, _ in globs]

    for r in range(sources):
        src = lax.rem(me - GROUP * r + seq_count, seq_count)
        for b in range(blocks):
            q = q_refs[r][pl.ds(b * BS, BS), :]
            tiles, ok = [], []
            if r == 0:
                start = aligned((lax.rem(me, GROUP) * blocks + b) * BS)
                window = key_rows[pl.ds(start, 3 * BS), :]
                tiles += [window[j * BS : (j + 1) * BS] for j in range(3)]
                at_first = (lax.rem(me, GROUP) > 0) if b == 0 else None
                at_last = (lax.rem(me, GROUP) < GROUP - 1) if b == blocks - 1 else None
                ok += [at_first, None, at_last]
            else:
                found = edge_block(src, b, blocks, seq_count, group, group_blocks)
                if found is not None:
                    tiles.append(key_rows[pl.ds(aligned(BS + found[0] * BS), BS), :])
                    ok.append(found[1])
            for j in range(2):
                tiles.append(glob_keys[j])
                ok.append(globs[j][1])
            for j in range(3):
                entry = table[((src * blocks + b) * heads + head) * 3 + j]
                place, inside = local_block(entry, group, group_blocks)
                tiles.append(key_rows[pl.ds(aligned(BS + place * BS), BS), :])
                ok.append(inside)
            scores = []
            for tile, flag in zip(tiles, ok):
                s = dot(tile, q, NT) * c2
                if flag is not None:
                    s = s - jnp.where(flag, 0.0, OFF)
                scores.append(s)
            top = scores[0]
            for s in scores[1:]:
                top = jnp.maximum(top, s)
            top = jnp.max(top, axis=0, keepdims=True)
            total = jnp.exp2(scores[0] - top)
            for s in scores[1:]:
                total = total + jnp.exp2(s - top)
            total = jnp.sum(total, axis=0, keepdims=True)
            out_ref[r, 0, pl.ds(b, 1), :] = top + jnp.log2(total)


def grads_kernel(sizes, head0, meta, table, *refs):
    seq_count, remote, blocks, heads = sizes
    sources = remote + 1
    tokens = blocks * BS
    refs = list(refs)

    def take(count):
        taken = refs[:count]
        del refs[:count]
        return taken

    q_refs, g_refs = take(sources), take(sources)
    k_refs, v_refs = take(GROUP), take(GROUP)
    norm_ref, dot_ref, norm_flat, dot_flat = take(4)
    (dq_own,) = take(1)
    dq_far = take(remote)
    dk_keep, dk_send, dv_keep, dv_send = take(4)
    q_rows, g_rows, k_rows, v_rows, dq_sum, dk_sum, dv_sum, listed = refs
    head = pl.program_id(0) + head0
    me = meta[0]
    pos = lax.rem(me, GROUP)
    group = me // GROUP
    group_blocks = GROUP * blocks
    c2 = SCALE * LOG2E

    @pl.when(pl.program_id(0) == 0)
    def _():
        zero_ends(k_rows)
        zero_ends(v_rows)

    place_group(me, k_refs, k_rows, tokens)
    place_group(me, v_refs, v_rows, tokens)
    for r in range(sources):
        q_rows[pl.ds(r * tokens, tokens), :] = q_refs[r][...]
        g_rows[pl.ds(r * tokens, tokens), :] = g_refs[r][...]
    dk_sum[...] = jnp.zeros_like(dk_sum)
    dv_sum[...] = jnp.zeros_like(dv_sum)
    dq_sum[...] = jnp.zeros_like(dq_sum)

    count = jnp.int32(0)

    def note(count, item, place, inside):
        listed[count] = item * group_blocks + place
        return count + inside.astype(jnp.int32)

    for r in range(sources):
        src = lax.rem(me - GROUP * r + seq_count, seq_count)
        for b in range(blocks):
            item = r * blocks + b
            for j in range(3):
                entry = table[((src * blocks + b) * heads + head) * 3 + j]
                count = note(count, item, *local_block(entry, group, group_blocks))
            if r > 0:
                found = edge_block(src, b, blocks, seq_count, group, group_blocks)
                if found is not None:
                    count = note(count, item, *found)
    for u in range(BATCH):
        listed[count + u] = 0

    def terms(q, g, k, v, norm, rdot):
        w = jnp.exp2(dot(k, q, NT) * c2 - norm)
        ds = w * (dot(v, g, NT) - rdot)
        wb, dsb = w.astype(jnp.bfloat16), ds.astype(jnp.bfloat16)
        return dot(dsb, k, TN), dot(dsb, q), dot(wb, g)

    lane = lax.broadcasted_iota(jnp.int32, (1, 2 * BS), 1)
    pairs = blocks // 2
    for t in range(pairs):
        rows = pl.ds(t * 2 * BS, 2 * BS)
        q, g = q_refs[0][rows, :], g_refs[0][rows, :]
        start = aligned((pos * blocks + 2 * t) * BS)
        span = pl.ds(start, 4 * BS)
        k, v = k_rows[span, :], v_rows[span, :]
        norm = norm_flat[0, 0, :, t * 2 * BS : (t + 1) * 2 * BS]
        rdot = dot_flat[0, 0, :, t * 2 * BS : (t + 1) * 2 * BS]
        first = jnp.where(lane < BS, norm, OFF)
        last = jnp.where(lane < BS, OFF, norm)
        if t == 0:
            first = first + jnp.where(pos > 0, 0.0, OFF)
        if t == pairs - 1:
            last = last + jnp.where(pos < GROUP - 1, 0.0, OFF)
        s = dot(k, q, NT) * c2
        w = jnp.concatenate(
            [
                jnp.exp2(s[:BS] - first),
                jnp.exp2(s[BS : 3 * BS] - norm),
                jnp.exp2(s[3 * BS :] - last),
            ],
            axis=0,
        )
        ds = w * (dot(v, g, NT) - rdot)
        wb, dsb = w.astype(jnp.bfloat16), ds.astype(jnp.bfloat16)
        dq_sum[rows, :] += dot(dsb, k, TN)
        dk_sum[span, :] += dot(dsb, q)
        dv_sum[span, :] += dot(wb, g)

    globs = [local_block(meta[1 + j], group, group_blocks) for j in range(2)]
    wide = 4 * BS if blocks % 4 == 0 else 2 * BS

    @pl.when(globs[0][1] | globs[1][1])
    def _():
        spans = [pl.ds(aligned(BS + p * BS), BS) for p, _ in globs]
        k = jnp.concatenate([k_rows[s, :] for s in spans], axis=0)
        v = jnp.concatenate([v_rows[s, :] for s in spans], axis=0)
        off = [jnp.where(inside, 0.0, OFF) for _, inside in globs]
        dk = jnp.zeros((2 * BS, DH), jnp.float32)
        dv = jnp.zeros((2 * BS, DH), jnp.float32)
        for r in range(sources):
            for t in range(tokens // wide):
                rows = pl.ds(r * tokens + t * wide, wide)
                q, g = q_rows[rows, :], g_rows[rows, :]
                norm = norm_flat[r, 0, :, t * wide : (t + 1) * wide]
                rdot = dot_flat[r, 0, :, t * wide : (t + 1) * wide]
                s = dot(k, q, NT) * c2
                w = jnp.concatenate(
                    [jnp.exp2(s[:BS] - (norm + off[0])), jnp.exp2(s[BS:] - (norm + off[1]))],
                    axis=0,
                )
                ds = w * (dot(v, g, NT) - rdot)
                wb, dsb = w.astype(jnp.bfloat16), ds.astype(jnp.bfloat16)
                dq_sum[rows, :] += dot(dsb, k, TN)
                dk = dk + dot(dsb, q)
                dv = dv + dot(wb, g)
        for j, span in enumerate(spans):
            dk_sum[span, :] += dk[j * BS : (j + 1) * BS]
            dv_sum[span, :] += dv[j * BS : (j + 1) * BS]

    def batch(step, carry):
        found = []
        for u in range(BATCH):
            i = step * BATCH + u
            code = listed[i]
            item = code // group_blocks
            place = code - item * group_blocks
            rows = pl.ds(aligned(item * BS), BS)
            span = pl.ds(aligned(BS + place * BS), BS)
            norm = norm_ref[0, pl.ds(item, 1), :] + jnp.where(i < count, 0.0, OFF)
            rdot = dot_ref[0, pl.ds(item, 1), :]
            found.append(
                (
                    rows,
                    span,
                    terms(
                        q_rows[rows, :], g_rows[rows, :], k_rows[span, :], v_rows[span, :], norm, rdot
                    ),
                )
            )
        for rows, span, (dq, dk, dv) in found:
            dq_sum[rows, :] += dq
            dk_sum[span, :] += dk
            dv_sum[span, :] += dv
        return carry

    lax.fori_loop(0, (count + BATCH - 1) // BATCH, batch, 0)

    dq_own[...] = dq_sum[pl.ds(0, tokens), :] * SCALE
    for r in range(remote):
        dq_far[r][...] = (dq_sum[pl.ds((r + 1) * tokens, tokens), :] * SCALE).astype(jnp.bfloat16)
    for j in range(GROUP):
        rows = pl.ds(aligned(BS + (pos ^ j) * tokens), tokens)
        for total, keep, send, axis, factor in (
            (dk_sum, dk_keep, dk_send, 1, SCALE),
            (dv_sum, dv_keep, dv_send, 2, 1.0),
        ):
            slot = (j >> 1) if axis == 1 else (j & 1)
            target = send if j & axis else keep
            part = total[rows, :]
            part = part * factor if factor != 1.0 else part
            target[slot] = part.astype(jnp.bfloat16)


def on_device(
    queries, key_states, value_states, forward_out, grad_out, random_blocks, global_blocks
):
    seq_count = lax.axis_size("seq")
    me = lax.axis_index("seq")
    tokens = queries.shape[0]
    blocks = tokens // BS
    heads = queries.shape[1] // DH
    sources = seq_count // GROUP
    remote = sources - 1
    sizes = (seq_count, remote, blocks, heads)

    def shift(array, r):
        pairs = [(i, (i + GROUP * r) % seq_count) for i in range(seq_count)]
        return lax.ppermute(array, "seq", pairs)

    def flip(array, j):
        return lax.ppermute(array, "seq", [(i, i ^ j) for i in range(seq_count)])

    def collect(array):
        across = flip(array, 2)
        return [array, flip(array, 1), across, flip(across, 1)]

    k_group = collect(key_states)
    q_all = [queries] + [shift(queries, r) for r in range(1, sources)]
    v_group = collect(value_states)
    g_all = [grad_out] + [shift(grad_out, r) for r in range(1, sources)]

    meta = jnp.concatenate([me.astype(jnp.int32)[None], global_blocks.astype(jnp.int32)])
    table = random_blocks.reshape(-1)

    def column(offset):
        return pl.BlockSpec((tokens, DH), lambda h, *_: (0, h + offset))

    padded_rows = (GROUP * tokens + 2 * BS, DH)
    partial_norms = pl.pallas_call(
        partial(norm_kernel, sizes),
        grid_spec=pltpu.PrefetchScalarGridSpec(
            num_scalar_prefetch=2,
            grid=(heads,),
            in_specs=[column(0)] * (sources + GROUP),
            out_specs=pl.BlockSpec((sources, 1, blocks, BS), lambda h, *_: (0, h, 0, 0)),
            scratch_shapes=[pltpu.VMEM(padded_rows, jnp.bfloat16)],
        ),
        out_shape=jax.ShapeDtypeStruct((sources, heads, blocks, BS), jnp.float32),
        compiler_params=pltpu.CompilerParams(vmem_limit_bytes=48 * 2**20),
        name="partial_norms",
    )(meta, table, *q_all, *k_group)

    row_dot = jnp.sum(
        grad_out.astype(jnp.float32).reshape(tokens, heads, DH)
        * forward_out.astype(jnp.float32).reshape(tokens, heads, DH),
        axis=-1,
    )
    row_dot = row_dot.reshape(blocks, BS, heads).transpose(2, 0, 1)

    mine = jnp.concatenate([partial_norms, row_dot[None]], axis=0)
    told = [mine] + [shift(mine, r) for r in range(1, sources)]
    norms, dots = [], []
    for r in range(sources):
        parts = jnp.stack([told[k][(r - k) % sources] for k in range(sources)])
        top = jnp.max(parts, axis=0)
        norms.append(top + jnp.log2(jnp.sum(jnp.exp2(parts - top), axis=0)))
        dots.append(told[r][sources])
    norms, dots = jnp.stack(norms), jnp.stack(dots)

    def by_item(array):
        return array.transpose(1, 0, 2, 3).reshape(heads, sources * blocks, BS)

    def flat(array):
        return array.reshape(sources, heads, 1, tokens)

    def gradients(head0, count):
        width = count * DH
        item_spec = pl.BlockSpec((1, sources * blocks, BS), lambda h, *_: (h + head0, 0, 0))
        flat_spec = pl.BlockSpec((sources, 1, 1, tokens), lambda h, *_: (0, h + head0, 0, 0))
        out_column = pl.BlockSpec((tokens, DH), lambda h, *_: (0, h))
        half_spec = pl.BlockSpec((GROUP // 2, tokens, DH), lambda h, *_: (0, 0, h))
        half_shape = jax.ShapeDtypeStruct((GROUP // 2, tokens, width), jnp.bfloat16)
        return pl.pallas_call(
            partial(grads_kernel, sizes, head0),
            grid_spec=pltpu.PrefetchScalarGridSpec(
                num_scalar_prefetch=2,
                grid=(count,),
                in_specs=[column(head0)] * (2 * sources + 2 * GROUP)
                + [item_spec] * 2
                + [flat_spec] * 2,
                out_specs=[out_column] * sources + [half_spec] * 4,
                scratch_shapes=[
                    pltpu.VMEM((sources * tokens, DH), jnp.bfloat16),
                    pltpu.VMEM((sources * tokens, DH), jnp.bfloat16),
                    pltpu.VMEM(padded_rows, jnp.bfloat16),
                    pltpu.VMEM(padded_rows, jnp.bfloat16),
                    pltpu.VMEM((sources * tokens, DH), jnp.float32),
                    pltpu.VMEM(padded_rows, jnp.float32),
                    pltpu.VMEM(padded_rows, jnp.float32),
                    pltpu.SMEM((sources * (3 * blocks + 2) + BATCH,), jnp.int32),
                ],
            ),
            out_shape=[jax.ShapeDtypeStruct((tokens, width), jnp.float32)]
            + [jax.ShapeDtypeStruct((tokens, width), jnp.bfloat16)] * remote
            + [half_shape] * 4,
            compiler_params=pltpu.CompilerParams(vmem_limit_bytes=48 * 2**20),
            name="gradients",
        )(
            meta,
            table,
            *q_all,
            *g_all,
            *k_group,
            *v_group,
            by_item(norms),
            by_item(dots),
            flat(norms),
            flat(dots),
        )

    def wide(array):
        return array.astype(jnp.float32)

    def reduced(keep, send, first, second):
        got = flip(send, first)
        onward = flip((wide(keep[1]) + wide(got[1])).astype(jnp.bfloat16), second)
        return (wide(keep[0]) + wide(got[0]) + wide(onward)).astype(jnp.bfloat16)

    def to_tokens(array):
        return lax.all_to_all(array, "head", split_axis=0, concat_axis=1, tiled=True)

    outs = gradients(0, heads)
    dq_own, dq_far = outs[0], outs[1:sources]
    dk_keep, dk_send, dv_keep, dv_send = outs[sources:]
    dk = to_tokens(reduced(dk_keep, dk_send, 1, 2))
    dv = to_tokens(reduced(dv_keep, dv_send, 2, 1))
    dq = dq_own
    for r in range(1, sources):
        dq = dq + wide(shift(dq_far[r - 1], -r))
    dq = to_tokens(dq.astype(jnp.bfloat16))
    return dq, dk, dv


def solution(mesh):
    return jax.shard_map(
        on_device,
        mesh=mesh,
        in_specs=(
            P("seq", "head"),
            P("seq", "head"),
            P("seq", "head"),
            P("seq", "head"),
            P("seq", "head"),
            P(None, "head", None),
            P(),
        ),
        out_specs=(P(("seq", "head"), None), P(("seq", "head"), None), P(("seq", "head"), None)),
        check_vma=False,
    )
```

```python
from functools import partial
import math

import jax
import jax.numpy as jnp
from jax import lax
from jax.experimental import pallas as pl
from jax.experimental.pallas import tpu as pltpu
from jax.sharding import PartitionSpec as P

DH = 128
BS = 64
GROUP = 4
BATCH = 8
CHUNKS = 2
JOINED = 4
LOG2E = math.log2(math.e)
SCALE = DH**-0.5
OFF = 1e30
NT = (((1,), (1,)), ((), ()))
TN = (((0,), (0,)), ((), ()))


def dot(a, b, dims=(((1,), (0,)), ((), ()))):
    return lax.dot_general(a, b, dims, preferred_element_type=jnp.float32)


def aligned(start):
    return pl.multiple_of(start, BS)


def place_group(me, key_refs, key_rows, tokens):
    for j, ref in enumerate(key_refs):
        start = aligned(BS + (lax.rem(me, GROUP) ^ j) * tokens)
        key_rows[pl.ds(start, tokens), :] = ref[...]


def zero_ends(key_rows):
    edge = jnp.zeros((BS, DH), key_rows.dtype)
    key_rows[pl.ds(0, BS), :] = edge
    key_rows[pl.ds(key_rows.shape[0] - BS, BS), :] = edge


def local_block(block, group, group_blocks):
    place = block - group * group_blocks
    inside = (place >= 0) & (place < group_blocks)
    return jnp.where(inside, place, 0), inside


def edge_block(src, b, blocks, seq_count, group, group_blocks):
    last = blocks - 1
    if b == 0:
        return local_block(src * blocks - 1, group, group_blocks)
    if b == last:
        return local_block((src + 1) * blocks, group, group_blocks)
    return None


def norm_kernel(sizes, meta, table, *refs):
    seq_count, remote, blocks, heads = sizes
    sources = remote + 1
    tokens = blocks * BS
    q_refs = refs[:sources]
    k_refs = refs[sources : sources + GROUP]
    out_ref, key_rows = refs[sources + GROUP :]
    head = pl.program_id(0)
    me = meta[0]
    group = me // GROUP
    group_blocks = GROUP * blocks
    c2 = SCALE * LOG2E

    @pl.when(head == 0)
    def _():
        zero_ends(key_rows)

    place_group(me, k_refs, key_rows, tokens)
    globs = [local_block(meta[1 + j], group, group_blocks) for j in range(2)]
    glob_keys = [key_rows[pl.ds(aligned(BS + p * BS), BS), :] for p, _ in globs]

    for r in range(sources):
        src = lax.rem(me - GROUP * r + seq_count, seq_count)
        for b in range(blocks):
            q = q_refs[r][pl.ds(b * BS, BS), :]
            tiles, ok = [], []
            if r == 0:
                start = aligned((lax.rem(me, GROUP) * blocks + b) * BS)
                window = key_rows[pl.ds(start, 3 * BS), :]
                tiles += [window[j * BS : (j + 1) * BS] for j in range(3)]
                at_first = (lax.rem(me, GROUP) > 0) if b == 0 else None
                at_last = (lax.rem(me, GROUP) < GROUP - 1) if b == blocks - 1 else None
                ok += [at_first, None, at_last]
            else:
                found = edge_block(src, b, blocks, seq_count, group, group_blocks)
                if found is not None:
                    tiles.append(key_rows[pl.ds(aligned(BS + found[0] * BS), BS), :])
                    ok.append(found[1])
            for j in range(2):
                tiles.append(glob_keys[j])
                ok.append(globs[j][1])
            for j in range(3):
                entry = table[((src * blocks + b) * heads + head) * 3 + j]
                place, inside = local_block(entry, group, group_blocks)
                tiles.append(key_rows[pl.ds(aligned(BS + place * BS), BS), :])
                ok.append(inside)
            scores = []
            for tile, flag in zip(tiles, ok):
                s = dot(tile, q, NT) * c2
                if flag is not None:
                    s = s - jnp.where(flag, 0.0, OFF)
                scores.append(s)
            top = scores[0]
            for s in scores[1:]:
                top = jnp.maximum(top, s)
            top = jnp.max(top, axis=0, keepdims=True)
            total = jnp.exp2(scores[0] - top)
            for s in scores[1:]:
                total = total + jnp.exp2(s - top)
            total = jnp.sum(total, axis=0, keepdims=True)
            out_ref[r, 0, pl.ds(b, 1), :] = top + jnp.log2(total)


def grads_kernel(sizes, head0, meta, table, *refs):
    seq_count, remote, blocks, heads = sizes
    sources = remote + 1
    tokens = blocks * BS
    refs = list(refs)

    def take(count):
        taken = refs[:count]
        del refs[:count]
        return taken

    q_refs, g_refs = take(sources), take(sources)
    k_refs, v_refs = take(GROUP), take(GROUP)
    norm_ref, dot_ref, norm_flat, dot_flat = take(4)
    (dq_own,) = take(1)
    dq_far = take(remote)
    dk_keep, dk_send, dv_keep, dv_send = take(4)
    q_rows, g_rows, k_rows, v_rows, dq_sum, dk_sum, dv_sum, listed = refs
    head = pl.program_id(0) + head0
    me = meta[0]
    pos = lax.rem(me, GROUP)
    group = me // GROUP
    group_blocks = GROUP * blocks
    c2 = SCALE * LOG2E

    @pl.when(pl.program_id(0) == 0)
    def _():
        zero_ends(k_rows)
        zero_ends(v_rows)

    place_group(me, k_refs, k_rows, tokens)
    place_group(me, v_refs, v_rows, tokens)
    for r in range(sources):
        q_rows[pl.ds(r * tokens, tokens), :] = q_refs[r][...]
        g_rows[pl.ds(r * tokens, tokens), :] = g_refs[r][...]
    dk_sum[...] = jnp.zeros_like(dk_sum)
    dv_sum[...] = jnp.zeros_like(dv_sum)
    dq_sum[...] = jnp.zeros_like(dq_sum)

    count = jnp.int32(0)

    def note(count, item, place, inside):
        listed[0, count] = item
        listed[1, count] = place
        return count + inside.astype(jnp.int32)

    for r in range(sources):
        src = lax.rem(me - GROUP * r + seq_count, seq_count)
        for b in range(blocks):
            item = r * blocks + b
            for j in range(3):
                entry = table[((src * blocks + b) * heads + head) * 3 + j]
                count = note(count, item, *local_block(entry, group, group_blocks))
            if r > 0:
                found = edge_block(src, b, blocks, seq_count, group, group_blocks)
                if found is not None:
                    count = note(count, item, *found)
    for u in range(BATCH):
        listed[0, count + u] = 0
        listed[1, count + u] = 0

    lane = lax.broadcasted_iota(jnp.int32, (1, 2 * BS), 1)
    pairs = blocks // 2
    for t in range(pairs):
        rows = pl.ds(t * 2 * BS, 2 * BS)
        q, g = q_refs[0][rows, :], g_refs[0][rows, :]
        start = aligned((pos * blocks + 2 * t) * BS)
        span = pl.ds(start, 4 * BS)
        k, v = k_rows[span, :], v_rows[span, :]
        norm = norm_flat[0, 0, :, t * 2 * BS : (t + 1) * 2 * BS]
        rdot = dot_flat[0, 0, :, t * 2 * BS : (t + 1) * 2 * BS]
        first = jnp.where(lane < BS, norm, OFF)
        last = jnp.where(lane < BS, OFF, norm)
        if t == 0:
            first = first + jnp.where(pos > 0, 0.0, OFF)
        if t == pairs - 1:
            last = last + jnp.where(pos < GROUP - 1, 0.0, OFF)
        s = dot(k, q, NT) * c2
        w = jnp.concatenate(
            [
                jnp.exp2(s[:BS] - first),
                jnp.exp2(s[BS : 3 * BS] - norm),
                jnp.exp2(s[3 * BS :] - last),
            ],
            axis=0,
        )
        ds = w * (dot(v, g, NT) - rdot)
        wb, dsb = w.astype(jnp.bfloat16), ds.astype(jnp.bfloat16)
        dq_sum[rows, :] += dot(dsb, k, TN)
        dk_sum[span, :] += dot(dsb, q)
        dv_sum[span, :] += dot(wb, g)

    globs = [local_block(meta[1 + j], group, group_blocks) for j in range(2)]
    wide = 4 * BS if blocks % 4 == 0 else 2 * BS

    @pl.when(globs[0][1] | globs[1][1])
    def _():
        spans = [pl.ds(aligned(BS + p * BS), BS) for p, _ in globs]
        k = jnp.concatenate([k_rows[s, :] for s in spans], axis=0)
        v = jnp.concatenate([v_rows[s, :] for s in spans], axis=0)
        off = [jnp.where(inside, 0.0, OFF) for _, inside in globs]
        dk = jnp.zeros((2 * BS, DH), jnp.float32)
        dv = jnp.zeros((2 * BS, DH), jnp.float32)
        for r in range(sources):
            for t in range(tokens // wide):
                rows = pl.ds(r * tokens + t * wide, wide)
                q, g = q_rows[rows, :], g_rows[rows, :]
                norm = norm_flat[r, 0, :, t * wide : (t + 1) * wide]
                rdot = dot_flat[r, 0, :, t * wide : (t + 1) * wide]
                s = dot(k, q, NT) * c2
                w = jnp.concatenate(
                    [jnp.exp2(s[:BS] - (norm + off[0])), jnp.exp2(s[BS:] - (norm + off[1]))],
                    axis=0,
                )
                ds = w * (dot(v, g, NT) - rdot)
                wb, dsb = w.astype(jnp.bfloat16), ds.astype(jnp.bfloat16)
                dq_sum[rows, :] += dot(dsb, k, TN)
                dk = dk + dot(dsb, q)
                dv = dv + dot(wb, g)
        for j, span in enumerate(spans):
            dk_sum[span, :] += dk[j * BS : (j + 1) * BS]
            dv_sum[span, :] += dv[j * BS : (j + 1) * BS]

    def batch(step, carry):
        done = []
        for first in range(0, BATCH, JOINED):
            rows, spans, norms, dots = [], [], [], []
            for u in range(first, first + JOINED):
                i = step * BATCH + u
                item = listed[0, i]
                rows.append(pl.ds(aligned(item * BS), BS))
                spans.append(pl.ds(aligned(BS + listed[1, i] * BS), BS))
                norms.append(norm_ref[0, pl.ds(item, 1), :] + jnp.where(i < count, 0.0, OFF))
                dots.append(dot_ref[0, pl.ds(item, 1), :])
            q = jnp.concatenate([q_rows[x, :] for x in rows], axis=0)
            g = jnp.concatenate([g_rows[x, :] for x in rows], axis=0)
            k = jnp.concatenate([k_rows[x, :] for x in spans], axis=0)
            v = jnp.concatenate([v_rows[x, :] for x in spans], axis=0)
            s, dw = dot(k, q, NT), dot(v, g, NT)
            w_diag, ds_diag = [], []
            for t in range(JOINED // 2):
                part = slice(t * 2 * BS, (t + 1) * 2 * BS)
                both = s[part, part] * c2
                w = jnp.concatenate(
                    [
                        jnp.exp2(both[:BS] - jnp.where(lane < BS, norms[2 * t], OFF)),
                        jnp.exp2(both[BS:] - jnp.where(lane < BS, OFF, norms[2 * t + 1])),
                    ],
                    axis=0,
                )
                ds = w * (dw[part, part] - jnp.where(lane < BS, dots[2 * t], dots[2 * t + 1]))
                w_diag.append(w.astype(jnp.bfloat16))
                ds_diag.append(ds.astype(jnp.bfloat16))

            def each(left, right, dims=(((1,), (0,)), ((), ()))):
                pieces = [
                    dot(x, right[t * 2 * BS : (t + 1) * 2 * BS], dims) for t, x in enumerate(left)
                ]
                return jnp.concatenate(pieces, axis=0)

            done.append((rows, spans, each(ds_diag, k, TN), each(ds_diag, q), each(w_diag, g)))
        for rows, spans, dq, dk, dv in done:
            for u in range(JOINED):
                part = slice(u * BS, (u + 1) * BS)
                dq_sum[rows[u], :] += dq[part]
                dk_sum[spans[u], :] += dk[part]
                dv_sum[spans[u], :] += dv[part]
        return carry

    lax.fori_loop(0, (count + BATCH - 1) // BATCH, batch, 0)

    dq_own[...] = dq_sum[pl.ds(0, tokens), :] * SCALE
    for r in range(remote):
        dq_far[r][...] = (dq_sum[pl.ds((r + 1) * tokens, tokens), :] * SCALE).astype(jnp.bfloat16)
    for j in range(GROUP):
        rows = pl.ds(aligned(BS + (pos ^ j) * tokens), tokens)
        for total, keep, send, axis, factor in (
            (dk_sum, dk_keep, dk_send, 1, SCALE),
            (dv_sum, dv_keep, dv_send, 2, 1.0),
        ):
            slot = (j >> 1) if axis == 1 else (j & 1)
            target = send if j & axis else keep
            part = total[rows, :]
            part = part * factor if factor != 1.0 else part
            target[slot] = part.astype(jnp.bfloat16)


def on_device(
    queries, key_states, value_states, forward_out, grad_out, random_blocks, global_blocks
):
    seq_count = lax.axis_size("seq")
    me = lax.axis_index("seq")
    tokens = queries.shape[0]
    blocks = tokens // BS
    heads = queries.shape[1] // DH
    sources = seq_count // GROUP
    remote = sources - 1
    sizes = (seq_count, remote, blocks, heads)

    def shift(array, r):
        pairs = [(i, (i + GROUP * r) % seq_count) for i in range(seq_count)]
        return lax.ppermute(array, "seq", pairs)

    def flip(array, j):
        return lax.ppermute(array, "seq", [(i, i ^ j) for i in range(seq_count)])

    def collect(array):
        across = flip(array, 2)
        return [array, flip(array, 1), across, flip(across, 1)]

    k_group = collect(key_states)
    q_all = [queries] + [shift(queries, r) for r in range(1, sources)]
    v_group = collect(value_states)
    g_all = [grad_out] + [shift(grad_out, r) for r in range(1, sources)]

    meta = jnp.concatenate([me.astype(jnp.int32)[None], global_blocks.astype(jnp.int32)])
    table = random_blocks.reshape(-1)

    def column(offset):
        return pl.BlockSpec((tokens, DH), lambda h, *_: (0, h + offset))

    padded_rows = (GROUP * tokens + 2 * BS, DH)
    partial_norms = pl.pallas_call(
        partial(norm_kernel, sizes),
        grid_spec=pltpu.PrefetchScalarGridSpec(
            num_scalar_prefetch=2,
            grid=(heads,),
            in_specs=[column(0)] * (sources + GROUP),
            out_specs=pl.BlockSpec((sources, 1, blocks, BS), lambda h, *_: (0, h, 0, 0)),
            scratch_shapes=[pltpu.VMEM(padded_rows, jnp.bfloat16)],
        ),
        out_shape=jax.ShapeDtypeStruct((sources, heads, blocks, BS), jnp.float32),
        compiler_params=pltpu.CompilerParams(vmem_limit_bytes=48 * 2**20),
        name="partial_norms",
    )(meta, table, *q_all, *k_group)

    row_dot = jnp.sum(
        grad_out.astype(jnp.float32).reshape(tokens, heads, DH)
        * forward_out.astype(jnp.float32).reshape(tokens, heads, DH),
        axis=-1,
    )
    row_dot = row_dot.reshape(blocks, BS, heads).transpose(2, 0, 1)

    mine = jnp.concatenate([partial_norms, row_dot[None]], axis=0)
    told = [mine] + [shift(mine, r) for r in range(1, sources)]
    norms, dots = [], []
    for r in range(sources):
        parts = jnp.stack([told[k][(r - k) % sources] for k in range(sources)])
        top = jnp.max(parts, axis=0)
        norms.append(top + jnp.log2(jnp.sum(jnp.exp2(parts - top), axis=0)))
        dots.append(told[r][sources])
    norms, dots = jnp.stack(norms), jnp.stack(dots)

    def by_item(array):
        array = array.transpose(1, 0, 2, 3).reshape(heads, sources * blocks, BS)
        return jnp.concatenate([array, array], axis=-1)

    def flat(array):
        return array.reshape(sources, heads, 1, tokens)

    def gradients(head0, count):
        width = count * DH
        item_spec = pl.BlockSpec((1, sources * blocks, 2 * BS), lambda h, *_: (h + head0, 0, 0))
        flat_spec = pl.BlockSpec((sources, 1, 1, tokens), lambda h, *_: (0, h + head0, 0, 0))
        out_column = pl.BlockSpec((tokens, DH), lambda h, *_: (0, h))
        half_spec = pl.BlockSpec((GROUP // 2, tokens, DH), lambda h, *_: (0, 0, h))
        half_shape = jax.ShapeDtypeStruct((GROUP // 2, tokens, width), jnp.bfloat16)
        return pl.pallas_call(
            partial(grads_kernel, sizes, head0),
            grid_spec=pltpu.PrefetchScalarGridSpec(
                num_scalar_prefetch=2,
                grid=(count,),
                in_specs=[column(head0)] * (2 * sources + 2 * GROUP)
                + [item_spec] * 2
                + [flat_spec] * 2,
                out_specs=[out_column] * sources + [half_spec] * 4,
                scratch_shapes=[
                    pltpu.VMEM((sources * tokens, DH), jnp.bfloat16),
                    pltpu.VMEM((sources * tokens, DH), jnp.bfloat16),
                    pltpu.VMEM(padded_rows, jnp.bfloat16),
                    pltpu.VMEM(padded_rows, jnp.bfloat16),
                    pltpu.VMEM((sources * tokens, DH), jnp.float32),
                    pltpu.VMEM(padded_rows, jnp.float32),
                    pltpu.VMEM(padded_rows, jnp.float32),
                    pltpu.SMEM((2, sources * (3 * blocks + 2) + BATCH), jnp.int32),
                ],
            ),
            out_shape=[jax.ShapeDtypeStruct((tokens, width), jnp.float32)]
            + [jax.ShapeDtypeStruct((tokens, width), jnp.bfloat16)] * remote
            + [half_shape] * 4,
            compiler_params=pltpu.CompilerParams(vmem_limit_bytes=48 * 2**20),
            name="gradients",
        )(
            meta,
            table,
            *q_all,
            *g_all,
            *k_group,
            *v_group,
            by_item(norms),
            by_item(dots),
            flat(norms),
            flat(dots),
        )

    def wide(array):
        return array.astype(jnp.float32)

    def reduced(keep, send, first, second):
        got = flip(send, first)
        onward = flip((wide(keep[1]) + wide(got[1])).astype(jnp.bfloat16), second)
        return (wide(keep[0]) + wide(got[0]) + wide(onward)).astype(jnp.bfloat16)

    def to_tokens(array):
        return lax.all_to_all(array, "head", split_axis=0, concat_axis=1, tiled=True)

    count = heads // CHUNKS
    dq_parts, dk_parts, dv_parts = [], [], []
    for c in range(CHUNKS):
        outs = gradients(c * count, count)
        dq, dq_far = outs[0], outs[1:sources]
        dk_keep, dk_send, dv_keep, dv_send = outs[sources:]
        for r in range(1, sources):
            dq = dq + wide(shift(dq_far[r - 1], -r))
        dq_parts.append(dq.astype(jnp.bfloat16))
        dk_parts.append(reduced(dk_keep, dk_send, 1, 2))
        dv_parts.append(reduced(dv_keep, dv_send, 2, 1))
    dq, dk, dv = (
        to_tokens(jnp.concatenate(parts, axis=1)) for parts in (dq_parts, dk_parts, dv_parts)
    )
    return dq, dk, dv


def solution(mesh):
    return jax.shard_map(
        on_device,
        mesh=mesh,
        in_specs=(
            P("seq", "head"),
            P("seq", "head"),
            P("seq", "head"),
            P("seq", "head"),
            P("seq", "head"),
            P(None, "head", None),
            P(),
        ),
        out_specs=(P(("seq", "head"), None), P(("seq", "head"), None), P(("seq", "head"), None)),
        check_vma=False,
    )
```

```python
from functools import partial
import math

import jax
import jax.numpy as jnp
from jax import lax
from jax.experimental import pallas as pl
from jax.experimental.pallas import tpu as pltpu
from jax.sharding import PartitionSpec as P

DH = 128
BS = 64
GROUP = 4
BATCH = 8
CHUNKS = 2
JOINED = 4
LOG2E = math.log2(math.e)
SCALE = DH**-0.5
OFF = 1e30
NT = (((1,), (1,)), ((), ()))
TN = (((0,), (0,)), ((), ()))


def dot(a, b, dims=(((1,), (0,)), ((), ()))):
    return lax.dot_general(a, b, dims, preferred_element_type=jnp.float32)


def aligned(start):
    return pl.multiple_of(start, BS)


def place_group(me, key_refs, key_rows, tokens):
    for j, ref in enumerate(key_refs):
        start = aligned(BS + (lax.rem(me, GROUP) ^ j) * tokens)
        key_rows[pl.ds(start, tokens), :] = ref[...]


def zero_ends(key_rows):
    edge = jnp.zeros((BS, DH), key_rows.dtype)
    key_rows[pl.ds(0, BS), :] = edge
    key_rows[pl.ds(key_rows.shape[0] - BS, BS), :] = edge


def local_block(block, group, group_blocks):
    place = block - group * group_blocks
    inside = (place >= 0) & (place < group_blocks)
    return jnp.where(inside, place, 0), inside


def edge_block(src, b, blocks, seq_count, group, group_blocks):
    last = blocks - 1
    if b == 0:
        return local_block(src * blocks - 1, group, group_blocks)
    if b == last:
        return local_block((src + 1) * blocks, group, group_blocks)
    return None


def norm_kernel(sizes, meta, table, *refs):
    seq_count, remote, blocks, heads = sizes
    sources = remote + 1
    tokens = blocks * BS
    q_refs = refs[:sources]
    k_refs = refs[sources : sources + GROUP]
    out_ref, key_rows = refs[sources + GROUP :]
    head = pl.program_id(0)
    me = meta[0]
    group = me // GROUP
    group_blocks = GROUP * blocks
    c2 = SCALE * LOG2E

    @pl.when(head == 0)
    def _():
        zero_ends(key_rows)

    place_group(me, k_refs, key_rows, tokens)
    globs = [local_block(meta[1 + j], group, group_blocks) for j in range(2)]
    glob_keys = [key_rows[pl.ds(aligned(BS + p * BS), BS), :] for p, _ in globs]

    for r in range(sources):
        src = lax.rem(me - GROUP * r + seq_count, seq_count)
        for b in range(blocks):
            q = q_refs[r][pl.ds(b * BS, BS), :]
            tiles, ok = [], []
            if r == 0:
                start = aligned((lax.rem(me, GROUP) * blocks + b) * BS)
                window = key_rows[pl.ds(start, 3 * BS), :]
                tiles += [window[j * BS : (j + 1) * BS] for j in range(3)]
                at_first = (lax.rem(me, GROUP) > 0) if b == 0 else None
                at_last = (lax.rem(me, GROUP) < GROUP - 1) if b == blocks - 1 else None
                ok += [at_first, None, at_last]
            else:
                found = edge_block(src, b, blocks, seq_count, group, group_blocks)
                if found is not None:
                    tiles.append(key_rows[pl.ds(aligned(BS + found[0] * BS), BS), :])
                    ok.append(found[1])
            for j in range(2):
                tiles.append(glob_keys[j])
                ok.append(globs[j][1])
            for j in range(3):
                entry = table[((src * blocks + b) * heads + head) * 3 + j]
                place, inside = local_block(entry, group, group_blocks)
                tiles.append(key_rows[pl.ds(aligned(BS + place * BS), BS), :])
                ok.append(inside)
            scores = []
            for tile, flag in zip(tiles, ok):
                s = dot(tile, q, NT) * c2
                if flag is not None:
                    s = s - jnp.where(flag, 0.0, OFF)
                scores.append(s)
            top = scores[0]
            for s in scores[1:]:
                top = jnp.maximum(top, s)
            top = jnp.max(top, axis=0, keepdims=True)
            total = jnp.exp2(scores[0] - top)
            for s in scores[1:]:
                total = total + jnp.exp2(s - top)
            total = jnp.sum(total, axis=0, keepdims=True)
            out_ref[r, 0, pl.ds(b, 1), :] = top + jnp.log2(total)


def grads_kernel(sizes, head0, meta, table, *refs):
    seq_count, remote, blocks, heads = sizes
    sources = remote + 1
    tokens = blocks * BS
    refs = list(refs)

    def take(count):
        taken = refs[:count]
        del refs[:count]
        return taken

    q_refs, g_refs = take(sources), take(sources)
    k_refs, v_refs = take(GROUP), take(GROUP)
    norm_ref, dot_ref, norm_flat, dot_flat = take(4)
    (dq_own,) = take(1)
    dq_far = take(remote)
    dk_keep, dk_send, dv_keep, dv_send = take(4)
    q_rows, g_rows, k_rows, v_rows, dq_sum, dk_sum, dv_sum, listed = refs
    head = pl.program_id(0) + head0
    me = meta[0]
    pos = lax.rem(me, GROUP)
    group = me // GROUP
    group_blocks = GROUP * blocks
    c2 = SCALE * LOG2E

    @pl.when(pl.program_id(0) == 0)
    def _():
        zero_ends(k_rows)
        zero_ends(v_rows)

    place_group(me, k_refs, k_rows, tokens)
    place_group(me, v_refs, v_rows, tokens)
    for r in range(sources):
        q_rows[pl.ds(r * tokens, tokens), :] = q_refs[r][...]
        g_rows[pl.ds(r * tokens, tokens), :] = g_refs[r][...]
    dk_sum[...] = jnp.zeros_like(dk_sum)
    dv_sum[...] = jnp.zeros_like(dv_sum)
    dq_sum[...] = jnp.zeros_like(dq_sum)

    count = jnp.int32(0)

    def note(count, item, place, inside):
        listed[0, count] = item
        listed[1, count] = place
        return count + inside.astype(jnp.int32)

    for r in range(sources):
        src = lax.rem(me - GROUP * r + seq_count, seq_count)
        for b in range(blocks):
            item = r * blocks + b
            for j in range(3):
                entry = table[((src * blocks + b) * heads + head) * 3 + j]
                count = note(count, item, *local_block(entry, group, group_blocks))
            if r > 0:
                found = edge_block(src, b, blocks, seq_count, group, group_blocks)
                if found is not None:
                    count = note(count, item, *found)
    for u in range(BATCH):
        listed[0, count + u] = 0
        listed[1, count + u] = 0

    lane = lax.broadcasted_iota(jnp.int32, (1, 2 * BS), 1)
    pairs = blocks // 2
    for t in range(pairs):
        rows = pl.ds(t * 2 * BS, 2 * BS)
        q, g = q_refs[0][rows, :], g_refs[0][rows, :]
        start = aligned((pos * blocks + 2 * t) * BS)
        span = pl.ds(start, 4 * BS)
        k, v = k_rows[span, :], v_rows[span, :]
        norm = norm_flat[0, 0, :, t * 2 * BS : (t + 1) * 2 * BS]
        rdot = dot_flat[0, 0, :, t * 2 * BS : (t + 1) * 2 * BS]
        first = jnp.where(lane < BS, norm, OFF)
        last = jnp.where(lane < BS, OFF, norm)
        if t == 0:
            first = first + jnp.where(pos > 0, 0.0, OFF)
        if t == pairs - 1:
            last = last + jnp.where(pos < GROUP - 1, 0.0, OFF)
        s = dot(k, q, NT) * c2
        w = jnp.concatenate(
            [
                jnp.exp2(s[:BS] - first),
                jnp.exp2(s[BS : 3 * BS] - norm),
                jnp.exp2(s[3 * BS :] - last),
            ],
            axis=0,
        )
        ds = w * (dot(v, g, NT) - rdot)
        wb, dsb = w.astype(jnp.bfloat16), ds.astype(jnp.bfloat16)
        dq_sum[rows, :] += dot(dsb, k, TN)
        dk_sum[span, :] += dot(dsb, q)
        dv_sum[span, :] += dot(wb, g)

    globs = [local_block(meta[1 + j], group, group_blocks) for j in range(2)]
    wide = 4 * BS if blocks % 4 == 0 else 2 * BS

    @pl.when(globs[0][1] | globs[1][1])
    def _():
        spans = [pl.ds(aligned(BS + p * BS), BS) for p, _ in globs]
        k = jnp.concatenate([k_rows[s, :] for s in spans], axis=0)
        v = jnp.concatenate([v_rows[s, :] for s in spans], axis=0)
        off = [jnp.where(inside, 0.0, OFF) for _, inside in globs]
        dk = jnp.zeros((2 * BS, DH), jnp.float32)
        dv = jnp.zeros((2 * BS, DH), jnp.float32)
        for r in range(sources):
            for t in range(tokens // wide):
                rows = pl.ds(r * tokens + t * wide, wide)
                q, g = q_rows[rows, :], g_rows[rows, :]
                norm = norm_flat[r, 0, :, t * wide : (t + 1) * wide]
                rdot = dot_flat[r, 0, :, t * wide : (t + 1) * wide]
                s = dot(k, q, NT) * c2
                w = jnp.concatenate(
                    [jnp.exp2(s[:BS] - (norm + off[0])), jnp.exp2(s[BS:] - (norm + off[1]))],
                    axis=0,
                )
                ds = w * (dot(v, g, NT) - rdot)
                wb, dsb = w.astype(jnp.bfloat16), ds.astype(jnp.bfloat16)
                dq_sum[rows, :] += dot(dsb, k, TN)
                dk = dk + dot(dsb, q)
                dv = dv + dot(wb, g)
        for j, span in enumerate(spans):
            dk_sum[span, :] += dk[j * BS : (j + 1) * BS]
            dv_sum[span, :] += dv[j * BS : (j + 1) * BS]

    def batch(step, carry):
        done = []
        for first in range(0, BATCH, JOINED):
            rows, spans, norms, dots = [], [], [], []
            for u in range(first, first + JOINED):
                i = step * BATCH + u
                item = listed[0, i]
                rows.append(pl.ds(aligned(item * BS), BS))
                spans.append(pl.ds(aligned(BS + listed[1, i] * BS), BS))
                norms.append(norm_ref[0, pl.ds(item, 1), :] + jnp.where(i < count, 0.0, OFF))
                dots.append(dot_ref[0, pl.ds(item, 1), :])
            q = jnp.concatenate([q_rows[x, :] for x in rows], axis=0)
            g = jnp.concatenate([g_rows[x, :] for x in rows], axis=0)
            k = jnp.concatenate([k_rows[x, :] for x in spans], axis=0)
            v = jnp.concatenate([v_rows[x, :] for x in spans], axis=0)
            s, dw = dot(k, q, NT), dot(v, g, NT)
            w_diag, ds_diag = [], []
            for t in range(JOINED // 2):
                part = slice(t * 2 * BS, (t + 1) * 2 * BS)
                both = s[part, part] * c2
                w = jnp.concatenate(
                    [
                        jnp.exp2(both[:BS] - jnp.where(lane < BS, norms[2 * t], OFF)),
                        jnp.exp2(both[BS:] - jnp.where(lane < BS, OFF, norms[2 * t + 1])),
                    ],
                    axis=0,
                )
                ds = w * (dw[part, part] - jnp.where(lane < BS, dots[2 * t], dots[2 * t + 1]))
                w_diag.append(w.astype(jnp.bfloat16))
                ds_diag.append(ds.astype(jnp.bfloat16))

            def each(left, right, dims=(((1,), (0,)), ((), ()))):
                pieces = [
                    dot(x, right[t * 2 * BS : (t + 1) * 2 * BS], dims) for t, x in enumerate(left)
                ]
                return jnp.concatenate(pieces, axis=0)

            done.append((rows, spans, each(ds_diag, k, TN), each(ds_diag, q), each(w_diag, g)))
        for rows, spans, dq, dk, dv in done:
            for u in range(JOINED):
                part = slice(u * BS, (u + 1) * BS)
                dq_sum[rows[u], :] += dq[part]
                dk_sum[spans[u], :] += dk[part]
                dv_sum[spans[u], :] += dv[part]
        return carry

    lax.fori_loop(0, (count + BATCH - 1) // BATCH, batch, 0)

    dq_own[...] = dq_sum[pl.ds(0, tokens), :] * SCALE
    for r in range(remote):
        dq_far[r][...] = (dq_sum[pl.ds((r + 1) * tokens, tokens), :] * SCALE).astype(jnp.bfloat16)
    for j in range(GROUP):
        rows = pl.ds(aligned(BS + (pos ^ j) * tokens), tokens)
        for total, keep, send, axis, factor in (
            (dk_sum, dk_keep, dk_send, 1, SCALE),
            (dv_sum, dv_keep, dv_send, 2, 1.0),
        ):
            slot = (j >> 1) if axis == 1 else (j & 1)
            target = send if j & axis else keep
            part = total[rows, :]
            part = part * factor if factor != 1.0 else part
            target[slot] = part.astype(jnp.bfloat16)


def on_device(
    queries, key_states, value_states, forward_out, grad_out, random_blocks, global_blocks
):
    seq_count = lax.axis_size("seq")
    me = lax.axis_index("seq")
    tokens = queries.shape[0]
    blocks = tokens // BS
    heads = queries.shape[1] // DH
    sources = seq_count // GROUP
    remote = sources - 1
    sizes = (seq_count, remote, blocks, heads)

    def shift(array, r):
        pairs = [(i, (i + GROUP * r) % seq_count) for i in range(seq_count)]
        return lax.ppermute(array, "seq", pairs)

    def flip(array, j):
        return lax.ppermute(array, "seq", [(i, i ^ j) for i in range(seq_count)])

    def after(array, other):
        return lax.optimization_barrier((array, other))[0]

    def whole(array, place=None):
        return [(array, place, 0)]

    count = heads // CHUNKS
    k_z = flip(key_states, 2)
    q_all = whole(queries)
    for r in range(1, sources):
        q_all += whole(shift(queries, r))
    kv_x = flip(jnp.stack([key_states, value_states]), 1)
    k_all = whole(key_states) + whole(kv_x, 0) + whole(k_z) + whole(flip(k_z, 1))

    v_chunks, previous = [], k_z
    g_all = whole(grad_out)
    for r in range(1, sources):
        g_all += whole(shift(after(grad_out, k_z), r))
    for c in range(CHUNKS):
        cut = slice(c * count * DH, (c + 1) * count * DH)
        v = after(value_states[:, cut], previous)
        own = [(value_states, None, c * count), (kv_x, 1, c * count)]
        if c == 0:
            v_z = flip(v, 2)
            v_all = own + [(v_z, None, 0), (flip(v_z, 1), None, 0)]
            previous = v_z
        else:
            v_z = flip(jnp.stack([v, kv_x[1][:, cut]]), 2)
            v_all = own + [(v_z, 0, 0), (v_z, 1, 0)]
            previous = v_z
        v_chunks.append(v_all)

    meta = jnp.concatenate([me.astype(jnp.int32)[None], global_blocks.astype(jnp.int32)])
    table = random_blocks.reshape(-1)

    def spec(operand, head0):
        _, place, first = operand
        if place is None:
            return pl.BlockSpec((tokens, DH), lambda h, *_: (0, h + head0 + first))
        return pl.BlockSpec((None, tokens, DH), lambda h, *_: (place, 0, h + head0 + first))

    def arrays(operands):
        return [array for array, _, _ in operands]

    padded_rows = (GROUP * tokens + 2 * BS, DH)
    partial_norms = pl.pallas_call(
        partial(norm_kernel, sizes),
        grid_spec=pltpu.PrefetchScalarGridSpec(
            num_scalar_prefetch=2,
            grid=(heads,),
            in_specs=[spec(x, 0) for x in q_all + k_all],
            out_specs=pl.BlockSpec((sources, 1, blocks, BS), lambda h, *_: (0, h, 0, 0)),
            scratch_shapes=[pltpu.VMEM(padded_rows, jnp.bfloat16)],
        ),
        out_shape=jax.ShapeDtypeStruct((sources, heads, blocks, BS), jnp.float32),
        compiler_params=pltpu.CompilerParams(vmem_limit_bytes=48 * 2**20),
        name="partial_norms",
    )(meta, table, *arrays(q_all + k_all))

    row_dot = jnp.sum(
        grad_out.astype(jnp.float32).reshape(tokens, heads, DH)
        * forward_out.astype(jnp.float32).reshape(tokens, heads, DH),
        axis=-1,
    )
    row_dot = row_dot.reshape(blocks, BS, heads).transpose(2, 0, 1)

    mine = jnp.concatenate([partial_norms, row_dot[None]], axis=0)
    told = [mine] + [shift(mine, r) for r in range(1, sources)]
    norms, dots = [], []
    for r in range(sources):
        parts = jnp.stack([told[k][(r - k) % sources] for k in range(sources)])
        top = jnp.max(parts, axis=0)
        norms.append(top + jnp.log2(jnp.sum(jnp.exp2(parts - top), axis=0)))
        dots.append(told[r][sources])
    norms, dots = jnp.stack(norms), jnp.stack(dots)

    def by_item(array):
        array = array.transpose(1, 0, 2, 3).reshape(heads, sources * blocks, BS)
        return jnp.concatenate([array, array], axis=-1)

    def flat(array):
        return array.reshape(sources, heads, 1, tokens)

    def gradients(c):
        head0 = c * count
        width = count * DH
        item_spec = pl.BlockSpec((1, sources * blocks, 2 * BS), lambda h, *_: (h + head0, 0, 0))
        flat_spec = pl.BlockSpec((sources, 1, 1, tokens), lambda h, *_: (0, h + head0, 0, 0))
        out_column = pl.BlockSpec((tokens, DH), lambda h, *_: (0, h))
        half_spec = pl.BlockSpec((GROUP // 2, tokens, DH), lambda h, *_: (0, 0, h))
        half_shape = jax.ShapeDtypeStruct((GROUP // 2, tokens, width), jnp.bfloat16)
        return pl.pallas_call(
            partial(grads_kernel, sizes, head0),
            grid_spec=pltpu.PrefetchScalarGridSpec(
                num_scalar_prefetch=2,
                grid=(count,),
                in_specs=[spec(x, head0) for x in q_all]
                + [spec(x, head0) for x in g_all]
                + [spec(x, head0) for x in k_all]
                + [spec(x, 0) for x in v_chunks[c]]
                + [item_spec] * 2
                + [flat_spec] * 2,
                out_specs=[out_column] * sources + [half_spec] * 4,
                scratch_shapes=[
                    pltpu.VMEM((sources * tokens, DH), jnp.bfloat16),
                    pltpu.VMEM((sources * tokens, DH), jnp.bfloat16),
                    pltpu.VMEM(padded_rows, jnp.bfloat16),
                    pltpu.VMEM(padded_rows, jnp.bfloat16),
                    pltpu.VMEM((sources * tokens, DH), jnp.float32),
                    pltpu.VMEM(padded_rows, jnp.float32),
                    pltpu.VMEM(padded_rows, jnp.float32),
                    pltpu.SMEM((2, sources * (3 * blocks + 2) + BATCH), jnp.int32),
                ],
            ),
            out_shape=[jax.ShapeDtypeStruct((tokens, width), jnp.float32)]
            + [jax.ShapeDtypeStruct((tokens, width), jnp.bfloat16)] * remote
            + [half_shape] * 4,
            compiler_params=pltpu.CompilerParams(vmem_limit_bytes=48 * 2**20),
            name="gradients",
        )(
            meta,
            table,
            *arrays(q_all + g_all + k_all + v_chunks[c]),
            by_item(norms),
            by_item(dots),
            flat(norms),
            flat(dots),
        )

    def wide(array):
        return array.astype(jnp.float32)

    def reduced(keep, send, first, second):
        got = flip(send, first)
        onward = flip((wide(keep[1]) + wide(got[1])).astype(jnp.bfloat16), second)
        return (wide(keep[0]) + wide(got[0]) + wide(onward)).astype(jnp.bfloat16)

    def to_tokens(array):
        return lax.all_to_all(array, "head", split_axis=0, concat_axis=1, tiled=True)

    dq_parts, dk_parts, dv_parts = [], [], []
    for c in range(CHUNKS):
        outs = gradients(c)
        dq, dq_far = outs[0], outs[1:sources]
        dk_keep, dk_send, dv_keep, dv_send = outs[sources:]
        for r in range(1, sources):
            dq = dq + wide(shift(dq_far[r - 1], -r))
        dq_parts.append(dq.astype(jnp.bfloat16))
        dk_parts.append(reduced(dk_keep, dk_send, 1, 2))
        dv_parts.append(reduced(dv_keep, dv_send, 2, 1))
    dq, dk, dv = (
        to_tokens(jnp.concatenate(parts, axis=1)) for parts in (dq_parts, dk_parts, dv_parts)
    )
    return dq, dk, dv


def solution(mesh):
    return jax.shard_map(
        on_device,
        mesh=mesh,
        in_specs=(
            P("seq", "head"),
            P("seq", "head"),
            P("seq", "head"),
            P("seq", "head"),
            P("seq", "head"),
            P(None, "head", None),
            P(),
        ),
        out_specs=(P(("seq", "head"), None), P(("seq", "head"), None), P(("seq", "head"), None)),
        check_vma=False,
    )
```

```python
from functools import partial
import math

import jax
import jax.numpy as jnp
from jax import lax
from jax.experimental import pallas as pl
from jax.experimental.pallas import tpu as pltpu
from jax.sharding import PartitionSpec as P

DH = 128
BS = 64
GROUP = 4
BATCH = 8
CUTS = (0.0, 0.5, 1.0)
JOINED = 4
LOG2E = math.log2(math.e)
SCALE = DH**-0.5
OFF = 1e30
NT = (((1,), (1,)), ((), ()))
TN = (((0,), (0,)), ((), ()))


def dot(a, b, dims=(((1,), (0,)), ((), ()))):
    return lax.dot_general(a, b, dims, preferred_element_type=jnp.float32)


def aligned(start):
    return pl.multiple_of(start, BS)


def place_group(me, key_refs, key_rows, tokens):
    for j, ref in enumerate(key_refs):
        start = aligned(BS + (lax.rem(me, GROUP) ^ j) * tokens)
        key_rows[pl.ds(start, tokens), :] = ref[...]


def zero_ends(key_rows):
    edge = jnp.zeros((BS, DH), key_rows.dtype)
    key_rows[pl.ds(0, BS), :] = edge
    key_rows[pl.ds(key_rows.shape[0] - BS, BS), :] = edge


def local_block(block, group, group_blocks):
    place = block - group * group_blocks
    inside = (place >= 0) & (place < group_blocks)
    return jnp.where(inside, place, 0), inside


def edge_block(src, b, blocks, seq_count, group, group_blocks):
    last = blocks - 1
    if b == 0:
        return local_block(src * blocks - 1, group, group_blocks)
    if b == last:
        return local_block((src + 1) * blocks, group, group_blocks)
    return None


def norm_kernel(sizes, meta, table, *refs):
    seq_count, remote, blocks, heads = sizes
    sources = remote + 1
    tokens = blocks * BS
    q_refs = refs[:sources]
    k_refs = refs[sources : sources + GROUP]
    out_ref, key_rows = refs[sources + GROUP :]
    head = pl.program_id(0)
    me = meta[0]
    group = me // GROUP
    group_blocks = GROUP * blocks
    c2 = SCALE * LOG2E

    @pl.when(head == 0)
    def _():
        zero_ends(key_rows)

    place_group(me, k_refs, key_rows, tokens)
    globs = [local_block(meta[1 + j], group, group_blocks) for j in range(2)]
    glob_keys = [key_rows[pl.ds(aligned(BS + p * BS), BS), :] for p, _ in globs]

    for r in range(sources):
        src = lax.rem(me - GROUP * r + seq_count, seq_count)
        for b in range(blocks):
            q = q_refs[r][pl.ds(b * BS, BS), :]
            tiles, ok = [], []
            if r == 0:
                start = aligned((lax.rem(me, GROUP) * blocks + b) * BS)
                window = key_rows[pl.ds(start, 3 * BS), :]
                tiles += [window[j * BS : (j + 1) * BS] for j in range(3)]
                at_first = (lax.rem(me, GROUP) > 0) if b == 0 else None
                at_last = (lax.rem(me, GROUP) < GROUP - 1) if b == blocks - 1 else None
                ok += [at_first, None, at_last]
            else:
                found = edge_block(src, b, blocks, seq_count, group, group_blocks)
                if found is not None:
                    tiles.append(key_rows[pl.ds(aligned(BS + found[0] * BS), BS), :])
                    ok.append(found[1])
            for j in range(2):
                tiles.append(glob_keys[j])
                ok.append(globs[j][1])
            for j in range(3):
                entry = table[((src * blocks + b) * heads + head) * 3 + j]
                place, inside = local_block(entry, group, group_blocks)
                tiles.append(key_rows[pl.ds(aligned(BS + place * BS), BS), :])
                ok.append(inside)
            scores = []
            for tile, flag in zip(tiles, ok):
                s = dot(tile, q, NT) * c2
                if flag is not None:
                    s = s - jnp.where(flag, 0.0, OFF)
                scores.append(s)
            top = scores[0]
            for s in scores[1:]:
                top = jnp.maximum(top, s)
            top = jnp.max(top, axis=0, keepdims=True)
            total = jnp.exp2(scores[0] - top)
            for s in scores[1:]:
                total = total + jnp.exp2(s - top)
            total = jnp.sum(total, axis=0, keepdims=True)
            out_ref[r, 0, pl.ds(b, 1), :] = top + jnp.log2(total)


def grads_kernel(sizes, head0, meta, table, *refs):
    seq_count, remote, blocks, heads = sizes
    sources = remote + 1
    tokens = blocks * BS
    refs = list(refs)

    def take(count):
        taken = refs[:count]
        del refs[:count]
        return taken

    q_refs, g_refs = take(sources), take(sources)
    k_refs, v_refs = take(GROUP), take(GROUP)
    norm_ref, dot_ref, norm_flat, dot_flat = take(4)
    (dq_own,) = take(1)
    dq_far = take(remote)
    dk_keep, dk_send, dv_keep, dv_send = take(4)
    q_rows, g_rows, k_rows, v_rows, dq_sum, dk_sum, dv_sum, w_kept, ds_kept, listed = refs
    head = pl.program_id(0) + head0
    me = meta[0]
    pos = lax.rem(me, GROUP)
    group = me // GROUP
    group_blocks = GROUP * blocks
    c2 = SCALE * LOG2E

    @pl.when(pl.program_id(0) == 0)
    def _():
        zero_ends(k_rows)
        zero_ends(v_rows)

    place_group(me, k_refs, k_rows, tokens)
    place_group(me, v_refs, v_rows, tokens)
    for r in range(sources):
        q_rows[pl.ds(r * tokens, tokens), :] = q_refs[r][...]
        g_rows[pl.ds(r * tokens, tokens), :] = g_refs[r][...]
    dk_sum[...] = jnp.zeros_like(dk_sum)
    dv_sum[...] = jnp.zeros_like(dv_sum)
    dq_sum[...] = jnp.zeros_like(dq_sum)

    count = jnp.int32(0)

    def note(count, item, place, inside):
        listed[0, count] = item
        listed[1, count] = place
        return count + inside.astype(jnp.int32)

    for r in range(sources):
        src = lax.rem(me - GROUP * r + seq_count, seq_count)
        for b in range(blocks):
            item = r * blocks + b
            for j in range(3):
                entry = table[((src * blocks + b) * heads + head) * 3 + j]
                count = note(count, item, *local_block(entry, group, group_blocks))
            if r > 0:
                found = edge_block(src, b, blocks, seq_count, group, group_blocks)
                if found is not None:
                    count = note(count, item, *found)
    for u in range(2 * BATCH):
        listed[0, count + u] = 0
        listed[1, count + u] = 0

    lane = lax.broadcasted_iota(jnp.int32, (1, 2 * BS), 1)

    globs = [local_block(meta[1 + j], group, group_blocks) for j in range(2)]
    wide = 4 * BS if blocks % 4 == 0 else 2 * BS

    @pl.when(globs[0][1] | globs[1][1])
    def _():
        spans = [pl.ds(aligned(BS + p * BS), BS) for p, _ in globs]
        k = jnp.concatenate([k_rows[s, :] for s in spans], axis=0)
        v = jnp.concatenate([v_rows[s, :] for s in spans], axis=0)
        off = [jnp.where(inside, 0.0, OFF) for _, inside in globs]
        dk = jnp.zeros((2 * BS, DH), jnp.float32)
        dv = jnp.zeros((2 * BS, DH), jnp.float32)
        for r in range(sources):
            for t in range(tokens // wide):
                rows = pl.ds(r * tokens + t * wide, wide)
                q, g = q_rows[rows, :], g_rows[rows, :]
                norm = norm_flat[r, 0, :, t * wide : (t + 1) * wide]
                rdot = dot_flat[r, 0, :, t * wide : (t + 1) * wide]
                s = dot(k, q, NT) * c2
                w = jnp.concatenate(
                    [jnp.exp2(s[:BS] - (norm + off[0])), jnp.exp2(s[BS:] - (norm + off[1]))],
                    axis=0,
                )
                ds = w * (dot(v, g, NT) - rdot)
                wb, dsb = w.astype(jnp.bfloat16), ds.astype(jnp.bfloat16)
                dq_sum[rows, :] += dot(dsb, k, TN)
                dk = dk + dot(dsb, q)
                dv = dv + dot(wb, g)
        for j, span in enumerate(spans):
            dk_sum[span, :] += dk[j * BS : (j + 1) * BS]
            dv_sum[span, :] += dv[j * BS : (j + 1) * BS]

    def places(step):
        rows, spans = [], []
        for u in range(BATCH):
            rows.append(pl.ds(aligned(listed[0, step * BATCH + u] * BS), BS))
            spans.append(pl.ds(aligned(BS + listed[1, step * BATCH + u] * BS), BS))
        return rows, spans

    def joined(ref, slices):
        return jnp.concatenate([ref[x, :] for x in slices], axis=0)

    def weigh(step):
        rows, spans = places(step)
        weighed = []
        for first in range(0, BATCH, JOINED):
            these = slice(first, first + JOINED)
            s = dot(joined(k_rows, spans[these]), joined(q_rows, rows[these]), NT)
            dw = dot(joined(v_rows, spans[these]), joined(g_rows, rows[these]), NT)
            for t in range(JOINED // 2):
                norms, dots = [], []
                for u in (first + 2 * t, first + 2 * t + 1):
                    item = listed[0, step * BATCH + u]
                    off = jnp.where(step * BATCH + u < count, 0.0, OFF)
                    norms.append(norm_ref[0, pl.ds(item, 1), :] + off)
                    dots.append(dot_ref[0, pl.ds(item, 1), :])
                part = slice(t * 2 * BS, (t + 1) * 2 * BS)
                both = s[part, part] * c2
                w = jnp.concatenate(
                    [
                        jnp.exp2(both[:BS] - jnp.where(lane < BS, norms[0], OFF)),
                        jnp.exp2(both[BS:] - jnp.where(lane < BS, OFF, norms[1])),
                    ],
                    axis=0,
                )
                ds = w * (dw[part, part] - jnp.where(lane < BS, dots[0], dots[1]))
                weighed.append((w.astype(jnp.bfloat16), ds.astype(jnp.bfloat16)))
        return weighed

    def keep_weighed(weighed):
        for t, (w, ds) in enumerate(weighed):
            w_kept[t], ds_kept[t] = w, ds

    def batch(step, carry):
        held = [(w_kept[t], ds_kept[t]) for t in range(BATCH // 2)]
        following = weigh(step + 1)
        rows, spans = places(step)
        done = []
        for t, (wb, dsb) in enumerate(held):
            pair = slice(2 * t, 2 * t + 2)
            q, g, k = joined(q_rows, rows[pair]), joined(g_rows, rows[pair]), joined(k_rows, spans[pair])
            done.append((dot(dsb, k, TN), dot(dsb, q), dot(wb, g)))
        keep_weighed(following)
        for u in range(BATCH):
            dq, dk, dv = done[u // 2]
            part = slice((u % 2) * BS, (u % 2 + 1) * BS)
            dq_sum[rows[u], :] += dq[part]
            dk_sum[spans[u], :] += dk[part]
            dv_sum[spans[u], :] += dv[part]
        return carry

    keep_weighed(weigh(0))
    pairs = blocks // 2
    for t in range(pairs):
        rows = pl.ds(t * 2 * BS, 2 * BS)
        q, g = q_refs[0][rows, :], g_refs[0][rows, :]
        start = aligned((pos * blocks + 2 * t) * BS)
        span = pl.ds(start, 4 * BS)
        k, v = k_rows[span, :], v_rows[span, :]
        norm = norm_flat[0, 0, :, t * 2 * BS : (t + 1) * 2 * BS]
        rdot = dot_flat[0, 0, :, t * 2 * BS : (t + 1) * 2 * BS]
        first = jnp.where(lane < BS, norm, OFF)
        last = jnp.where(lane < BS, OFF, norm)
        if t == 0:
            first = first + jnp.where(pos > 0, 0.0, OFF)
        if t == pairs - 1:
            last = last + jnp.where(pos < GROUP - 1, 0.0, OFF)
        s = dot(k, q, NT) * c2
        w = jnp.concatenate(
            [
                jnp.exp2(s[:BS] - first),
                jnp.exp2(s[BS : 3 * BS] - norm),
                jnp.exp2(s[3 * BS :] - last),
            ],
            axis=0,
        )
        ds = w * (dot(v, g, NT) - rdot)
        wb, dsb = w.astype(jnp.bfloat16), ds.astype(jnp.bfloat16)
        dq_sum[rows, :] += dot(dsb, k, TN)
        dk_sum[span, :] += dot(dsb, q)
        dv_sum[span, :] += dot(wb, g)

    lax.fori_loop(0, (count + BATCH - 1) // BATCH, batch, 0)

    dq_own[...] = dq_sum[pl.ds(0, tokens), :] * SCALE
    for r in range(remote):
        dq_far[r][...] = (dq_sum[pl.ds((r + 1) * tokens, tokens), :] * SCALE).astype(jnp.bfloat16)
    for j in range(GROUP):
        rows = pl.ds(aligned(BS + (pos ^ j) * tokens), tokens)
        for total, keep, send, axis, factor in (
            (dk_sum, dk_keep, dk_send, 1, SCALE),
            (dv_sum, dv_keep, dv_send, 2, 1.0),
        ):
            slot = (j >> 1) if axis == 1 else (j & 1)
            target = send if j & axis else keep
            part = total[rows, :]
            part = part * factor if factor != 1.0 else part
            target[slot] = part.astype(jnp.bfloat16)


def on_device(
    queries, key_states, value_states, forward_out, grad_out, random_blocks, global_blocks
):
    seq_count = lax.axis_size("seq")
    me = lax.axis_index("seq")
    tokens = queries.shape[0]
    blocks = tokens // BS
    heads = queries.shape[1] // DH
    sources = seq_count // GROUP
    remote = sources - 1
    sizes = (seq_count, remote, blocks, heads)

    def shift(array, r):
        pairs = [(i, (i + GROUP * r) % seq_count) for i in range(seq_count)]
        return lax.ppermute(array, "seq", pairs)

    def flip(array, j):
        return lax.ppermute(array, "seq", [(i, i ^ j) for i in range(seq_count)])

    def after(array, other):
        return lax.optimization_barrier((array, other))[0]

    def whole(array, place=None):
        return [(array, place, 0)]

    cuts = [round(heads * x) for x in CUTS]
    chunks = list(zip(cuts[:-1], cuts[1:]))
    k_z = flip(key_states, 2)
    q_all = whole(queries)
    for r in range(1, sources):
        q_all += whole(shift(queries, r))
    kv_x = flip(jnp.stack([key_states, value_states]), 1)
    k_all = whole(key_states) + whole(kv_x, 0) + whole(k_z) + whole(flip(k_z, 1))

    v_chunks, previous = [], k_z
    g_all = whole(grad_out)
    for r in range(1, sources):
        g_all += whole(shift(grad_out, r))
    for c, (low, high) in enumerate(chunks):
        cut = slice(low * DH, high * DH)
        v = after(value_states[:, cut], previous)
        own = [(value_states, None, low), (kv_x, 1, low)]
        if c == 0:
            v_z = flip(v, 2)
            v_all = own + [(v_z, None, 0), (flip(v_z, 1), None, 0)]
            previous = v_z
        else:
            v_z = flip(jnp.stack([v, kv_x[1][:, cut]]), 2)
            v_all = own + [(v_z, 0, 0), (v_z, 1, 0)]
            previous = v_z
        v_chunks.append(v_all)

    meta = jnp.concatenate([me.astype(jnp.int32)[None], global_blocks.astype(jnp.int32)])
    table = random_blocks.reshape(-1)

    def spec(operand, head0):
        _, place, first = operand
        if place is None:
            return pl.BlockSpec((tokens, DH), lambda h, *_: (0, h + head0 + first))
        return pl.BlockSpec((None, tokens, DH), lambda h, *_: (place, 0, h + head0 + first))

    def arrays(operands):
        return [array for array, _, _ in operands]

    padded_rows = (GROUP * tokens + 2 * BS, DH)
    partial_norms = pl.pallas_call(
        partial(norm_kernel, sizes),
        grid_spec=pltpu.PrefetchScalarGridSpec(
            num_scalar_prefetch=2,
            grid=(heads,),
            in_specs=[spec(x, 0) for x in q_all + k_all],
            out_specs=pl.BlockSpec((sources, 1, blocks, BS), lambda h, *_: (0, h, 0, 0)),
            scratch_shapes=[pltpu.VMEM(padded_rows, jnp.bfloat16)],
        ),
        out_shape=jax.ShapeDtypeStruct((sources, heads, blocks, BS), jnp.float32),
        compiler_params=pltpu.CompilerParams(vmem_limit_bytes=48 * 2**20),
        name="partial_norms",
    )(meta, table, *arrays(q_all + k_all))

    row_dot = jnp.sum(
        grad_out.astype(jnp.float32).reshape(tokens, heads, DH)
        * forward_out.astype(jnp.float32).reshape(tokens, heads, DH),
        axis=-1,
    )
    row_dot = row_dot.reshape(blocks, BS, heads).transpose(2, 0, 1)

    mine = jnp.concatenate([partial_norms, row_dot[None]], axis=0)
    told = [mine] + [shift(mine, r) for r in range(1, sources)]
    norms, dots = [], []
    for r in range(sources):
        parts = jnp.stack([told[k][(r - k) % sources] for k in range(sources)])
        top = jnp.max(parts, axis=0)
        norms.append(top + jnp.log2(jnp.sum(jnp.exp2(parts - top), axis=0)))
        dots.append(told[r][sources])
    norms, dots = jnp.stack(norms), jnp.stack(dots)

    def by_item(array):
        array = array.transpose(1, 0, 2, 3).reshape(heads, sources * blocks, BS)
        return jnp.concatenate([array, array], axis=-1)

    def flat(array):
        return array.reshape(sources, heads, 1, tokens)

    def gradients(c):
        head0, count = chunks[c][0], chunks[c][1] - chunks[c][0]
        width = count * DH
        item_spec = pl.BlockSpec((1, sources * blocks, 2 * BS), lambda h, *_: (h + head0, 0, 0))
        flat_spec = pl.BlockSpec((sources, 1, 1, tokens), lambda h, *_: (0, h + head0, 0, 0))
        out_column = pl.BlockSpec((tokens, DH), lambda h, *_: (0, h))
        half_spec = pl.BlockSpec((GROUP // 2, tokens, DH), lambda h, *_: (0, 0, h))
        half_shape = jax.ShapeDtypeStruct((GROUP // 2, tokens, width), jnp.bfloat16)
        return pl.pallas_call(
            partial(grads_kernel, sizes, head0),
            grid_spec=pltpu.PrefetchScalarGridSpec(
                num_scalar_prefetch=2,
                grid=(count,),
                in_specs=[spec(x, head0) for x in q_all]
                + [spec(x, head0) for x in g_all]
                + [spec(x, head0) for x in k_all]
                + [spec(x, 0) for x in v_chunks[c]]
                + [item_spec] * 2
                + [flat_spec] * 2,
                out_specs=[out_column] * sources + [half_spec] * 4,
                scratch_shapes=[
                    pltpu.VMEM((sources * tokens, DH), jnp.bfloat16),
                    pltpu.VMEM((sources * tokens, DH), jnp.bfloat16),
                    pltpu.VMEM(padded_rows, jnp.bfloat16),
                    pltpu.VMEM(padded_rows, jnp.bfloat16),
                    pltpu.VMEM((sources * tokens, DH), jnp.float32),
                    pltpu.VMEM(padded_rows, jnp.float32),
                    pltpu.VMEM(padded_rows, jnp.float32),
                    pltpu.VMEM((BATCH // 2, 2 * BS, 2 * BS), jnp.bfloat16),
                    pltpu.VMEM((BATCH // 2, 2 * BS, 2 * BS), jnp.bfloat16),
                    pltpu.SMEM((2, sources * (3 * blocks + 2) + 2 * BATCH), jnp.int32),
                ],
            ),
            out_shape=[jax.ShapeDtypeStruct((tokens, width), jnp.float32)]
            + [jax.ShapeDtypeStruct((tokens, width), jnp.bfloat16)] * remote
            + [half_shape] * 4,
            compiler_params=pltpu.CompilerParams(vmem_limit_bytes=48 * 2**20),
            name="gradients",
        )(
            meta,
            table,
            *arrays(q_all + g_all + k_all + v_chunks[c]),
            by_item(norms),
            by_item(dots),
            flat(norms),
            flat(dots),
        )

    def wide(array):
        return array.astype(jnp.float32)

    def reduced(keep, send, first, second):
        got = flip(send, first)
        onward = flip((wide(keep[1]) + wide(got[1])).astype(jnp.bfloat16), second)
        return (wide(keep[0]) + wide(got[0]) + wide(onward)).astype(jnp.bfloat16)

    def to_tokens(array):
        return lax.all_to_all(array, "head", split_axis=0, concat_axis=1, tiled=True)

    dq_parts, dk_parts, dv_parts = [], [], []
    for c in range(len(chunks)):
        outs = gradients(c)
        dq, dq_far = outs[0], outs[1:sources]
        dk_keep, dk_send, dv_keep, dv_send = outs[sources:]
        for r in range(1, sources):
            dq = dq + wide(shift(dq_far[r - 1], -r))
        dq_parts.append(dq.astype(jnp.bfloat16))
        dk_parts.append(reduced(dk_keep, dk_send, 1, 2))
        dv_parts.append(reduced(dv_keep, dv_send, 2, 1))
    dq, dk, dv = (
        to_tokens(jnp.concatenate(parts, axis=1)) for parts in (dq_parts, dk_parts, dv_parts)
    )
    return dq, dk, dv


def solution(mesh):
    return jax.shard_map(
        on_device,
        mesh=mesh,
        in_specs=(
            P("seq", "head"),
            P("seq", "head"),
            P("seq", "head"),
            P("seq", "head"),
            P("seq", "head"),
            P(None, "head", None),
            P(),
        ),
        out_specs=(P(("seq", "head"), None), P(("seq", "head"), None), P(("seq", "head"), None)),
        check_vma=False,
    )
```

```python
from functools import partial
import math

import jax
import jax.numpy as jnp
from jax import lax
from jax.experimental import pallas as pl
from jax.experimental.pallas import tpu as pltpu
from jax.sharding import PartitionSpec as P

DH = 128
BS = 64
GROUP = 4
BATCH = 8
CUTS = (0.0, 0.5, 1.0)
JOINED = 4
LOG2E = math.log2(math.e)
SCALE = DH**-0.5
OFF = 1e30
NT = (((1,), (1,)), ((), ()))
TN = (((0,), (0,)), ((), ()))


def dot(a, b, dims=(((1,), (0,)), ((), ()))):
    return lax.dot_general(a, b, dims, preferred_element_type=jnp.float32)


def aligned(start):
    return pl.multiple_of(start, BS)


def place_group(me, key_refs, key_rows, tokens):
    for j, ref in enumerate(key_refs):
        start = aligned(BS + (lax.rem(me, GROUP) ^ j) * tokens)
        key_rows[pl.ds(start, tokens), :] = ref[...]


def zero_ends(key_rows):
    edge = jnp.zeros((BS, DH), key_rows.dtype)
    key_rows[pl.ds(0, BS), :] = edge
    key_rows[pl.ds(key_rows.shape[0] - BS, BS), :] = edge


def local_block(block, group, group_blocks):
    place = block - group * group_blocks
    inside = (place >= 0) & (place < group_blocks)
    return jnp.where(inside, place, 0), inside


def edge_block(src, b, blocks, seq_count, group, group_blocks):
    last = blocks - 1
    if b == 0:
        return local_block(src * blocks - 1, group, group_blocks)
    if b == last:
        return local_block((src + 1) * blocks, group, group_blocks)
    return None


def norm_kernel(sizes, meta, table, *refs):
    seq_count, remote, blocks, heads = sizes
    sources = remote + 1
    tokens = blocks * BS
    q_refs = refs[:sources]
    k_refs = refs[sources : sources + GROUP]
    out_ref, key_rows = refs[sources + GROUP :]
    head = pl.program_id(0)
    me = meta[0]
    group = me // GROUP
    group_blocks = GROUP * blocks
    c2 = SCALE * LOG2E

    @pl.when(head == 0)
    def _():
        zero_ends(key_rows)

    place_group(me, k_refs, key_rows, tokens)
    globs = [local_block(meta[1 + j], group, group_blocks) for j in range(2)]
    glob_keys = [key_rows[pl.ds(aligned(BS + p * BS), BS), :] for p, _ in globs]

    pos = lax.rem(me, GROUP)
    lane = lax.broadcasted_iota(jnp.int32, (1, 2 * BS), 1)
    for r in range(sources):
        src = lax.rem(me - GROUP * r + seq_count, seq_count)
        for t in range(blocks // 2):
            q = q_refs[r][pl.ds(t * 2 * BS, 2 * BS), :]
            tiles, off = [], []
            if r == 0:
                start = aligned((pos * blocks + 2 * t) * BS)
                tiles.append(key_rows[pl.ds(start, 4 * BS), :])
                first = jnp.where(pos > 0, 0.0, OFF) if t == 0 else 0.0
                last = jnp.where(pos < GROUP - 1, 0.0, OFF) if t == blocks // 2 - 1 else 0.0
                off += [(first, OFF), None, None, (OFF, last)]
            for j in range(2):
                tiles.append(glob_keys[j])
                here = jnp.where(globs[j][1], 0.0, OFF)
                off.append((here, here))
            for u in range(2):
                b = 2 * t + u
                found = [
                    local_block(table[((src * blocks + b) * heads + head) * 3 + j], group, group_blocks)
                    for j in range(3)
                ]
                edge = edge_block(src, b, blocks, seq_count, group, group_blocks)
                if r > 0 and edge is not None:
                    found.append(edge)
                for place, inside in found:
                    tiles.append(key_rows[pl.ds(aligned(BS + place * BS), BS), :])
                    here = jnp.where(inside, 0.0, OFF)
                    off.append((here, OFF) if u == 0 else (OFF, here))
            products = dot(jnp.concatenate(tiles, axis=0), q, NT)
            scores = []
            for j, pair in enumerate(off):
                s = products[j * BS : (j + 1) * BS] * c2
                if pair is not None:
                    s = s - jnp.where(lane < BS, pair[0], pair[1])
                scores.append(s)
            top = scores[0]
            for s in scores[1:]:
                top = jnp.maximum(top, s)
            top = jnp.max(top, axis=0, keepdims=True)
            total = jnp.exp2(scores[0] - top)
            for s in scores[1:]:
                total = total + jnp.exp2(s - top)
            found = top + jnp.log2(jnp.sum(total, axis=0, keepdims=True))
            out_ref[r, 0, pl.ds(2 * t, 1), :] = found[:, :BS]
            out_ref[r, 0, pl.ds(2 * t + 1, 1), :] = found[:, BS:]


def grads_kernel(sizes, head0, meta, table, *refs):
    seq_count, remote, blocks, heads = sizes
    sources = remote + 1
    tokens = blocks * BS
    refs = list(refs)

    def take(count):
        taken = refs[:count]
        del refs[:count]
        return taken

    q_refs, g_refs = take(sources), take(sources)
    k_refs, v_refs = take(GROUP), take(GROUP)
    norm_ref, dot_ref, norm_flat, dot_flat = take(4)
    (dq_own,) = take(1)
    dq_far = take(remote)
    dk_keep, dk_send, dv_keep, dv_send = take(4)
    q_rows, g_rows, k_rows, v_rows, dq_sum, dk_sum, dv_sum, w_kept, ds_kept, listed = refs
    head = pl.program_id(0) + head0
    me = meta[0]
    pos = lax.rem(me, GROUP)
    group = me // GROUP
    group_blocks = GROUP * blocks
    c2 = SCALE * LOG2E

    @pl.when(pl.program_id(0) == 0)
    def _():
        zero_ends(k_rows)
        zero_ends(v_rows)

    place_group(me, k_refs, k_rows, tokens)
    place_group(me, v_refs, v_rows, tokens)
    for r in range(sources):
        q_rows[pl.ds(r * tokens, tokens), :] = q_refs[r][...]
        g_rows[pl.ds(r * tokens, tokens), :] = g_refs[r][...]
    dk_sum[...] = jnp.zeros_like(dk_sum)
    dv_sum[...] = jnp.zeros_like(dv_sum)
    dq_sum[...] = jnp.zeros_like(dq_sum)

    count = jnp.int32(0)

    def note(count, item, place, inside):
        listed[0, count] = item
        listed[1, count] = place
        return count + inside.astype(jnp.int32)

    for r in range(sources):
        src = lax.rem(me - GROUP * r + seq_count, seq_count)
        for b in range(blocks):
            item = r * blocks + b
            for j in range(3):
                entry = table[((src * blocks + b) * heads + head) * 3 + j]
                count = note(count, item, *local_block(entry, group, group_blocks))
            if r > 0:
                found = edge_block(src, b, blocks, seq_count, group, group_blocks)
                if found is not None:
                    count = note(count, item, *found)
    for u in range(2 * BATCH):
        listed[0, count + u] = 0
        listed[1, count + u] = 0

    lane = lax.broadcasted_iota(jnp.int32, (1, 2 * BS), 1)

    globs = [local_block(meta[1 + j], group, group_blocks) for j in range(2)]
    wide = tokens

    spans = [pl.ds(aligned(BS + p * BS), BS) for p, _ in globs]
    k = jnp.concatenate([k_rows[s, :] for s in spans], axis=0)
    v = jnp.concatenate([v_rows[s, :] for s in spans], axis=0)
    off = [jnp.where(inside, 0.0, OFF) for _, inside in globs]
    dk = jnp.zeros((2 * BS, DH), jnp.float32)
    dv = jnp.zeros((2 * BS, DH), jnp.float32)
    for r in range(sources):
        for t in range(tokens // wide):
            rows = pl.ds(r * tokens + t * wide, wide)
            q, g = q_rows[rows, :], g_rows[rows, :]
            norm = norm_flat[r, 0, :, t * wide : (t + 1) * wide]
            rdot = dot_flat[r, 0, :, t * wide : (t + 1) * wide]
            s = dot(k, q, NT) * c2
            w = jnp.concatenate(
                [jnp.exp2(s[:BS] - (norm + off[0])), jnp.exp2(s[BS:] - (norm + off[1]))],
                axis=0,
            )
            ds = w * (dot(v, g, NT) - rdot)
            wb, dsb = w.astype(jnp.bfloat16), ds.astype(jnp.bfloat16)
            dq_sum[rows, :] += dot(dsb, k, TN)
            dk = dk + dot(dsb, q)
            dv = dv + dot(wb, g)
    for j, span in enumerate(spans):
        dk_sum[span, :] += dk[j * BS : (j + 1) * BS]
        dv_sum[span, :] += dv[j * BS : (j + 1) * BS]

    def places(step):
        rows, spans = [], []
        for u in range(BATCH):
            rows.append(pl.ds(aligned(listed[0, step * BATCH + u] * BS), BS))
            spans.append(pl.ds(aligned(BS + listed[1, step * BATCH + u] * BS), BS))
        return rows, spans

    def joined(ref, slices):
        return jnp.concatenate([ref[x, :] for x in slices], axis=0)

    def weigh(step):
        rows, spans = places(step)
        weighed = []
        for first in range(0, BATCH, JOINED):
            these = slice(first, first + JOINED)
            s = dot(joined(k_rows, spans[these]), joined(q_rows, rows[these]), NT)
            dw = dot(joined(v_rows, spans[these]), joined(g_rows, rows[these]), NT)
            for t in range(JOINED // 2):
                norms, dots = [], []
                for u in (first + 2 * t, first + 2 * t + 1):
                    item = listed[0, step * BATCH + u]
                    off = jnp.where(step * BATCH + u < count, 0.0, OFF)
                    norms.append(norm_ref[0, pl.ds(item, 1), :] + off)
                    dots.append(dot_ref[0, pl.ds(item, 1), :])
                part = slice(t * 2 * BS, (t + 1) * 2 * BS)
                both = s[part, part] * c2
                w = jnp.concatenate(
                    [
                        jnp.exp2(both[:BS] - jnp.where(lane < BS, norms[0], OFF)),
                        jnp.exp2(both[BS:] - jnp.where(lane < BS, OFF, norms[1])),
                    ],
                    axis=0,
                )
                ds = w * (dw[part, part] - jnp.where(lane < BS, dots[0], dots[1]))
                weighed.append((w.astype(jnp.bfloat16), ds.astype(jnp.bfloat16)))
        return weighed

    def keep_weighed(weighed):
        for t, (w, ds) in enumerate(weighed):
            w_kept[t], ds_kept[t] = w, ds

    def batch(step, carry):
        held = [(w_kept[t], ds_kept[t]) for t in range(BATCH // 2)]
        following = weigh(step + 1)
        rows, spans = places(step)
        done = []
        for t, (wb, dsb) in enumerate(held):
            pair = slice(2 * t, 2 * t + 2)
            q, g, k = joined(q_rows, rows[pair]), joined(g_rows, rows[pair]), joined(k_rows, spans[pair])
            done.append((dot(dsb, k, TN), dot(dsb, q), dot(wb, g)))
        keep_weighed(following)
        for u in range(BATCH):
            dq, dk, dv = done[u // 2]
            part = slice((u % 2) * BS, (u % 2 + 1) * BS)
            dq_sum[rows[u], :] += dq[part]
            dk_sum[spans[u], :] += dk[part]
            dv_sum[spans[u], :] += dv[part]
        return carry

    keep_weighed(weigh(0))
    pairs = blocks // 2
    for t in range(pairs):
        rows = pl.ds(t * 2 * BS, 2 * BS)
        q, g = q_refs[0][rows, :], g_refs[0][rows, :]
        start = aligned((pos * blocks + 2 * t) * BS)
        span = pl.ds(start, 4 * BS)
        k, v = k_rows[span, :], v_rows[span, :]
        norm = norm_flat[0, 0, :, t * 2 * BS : (t + 1) * 2 * BS]
        rdot = dot_flat[0, 0, :, t * 2 * BS : (t + 1) * 2 * BS]
        first = jnp.where(lane < BS, norm, OFF)
        last = jnp.where(lane < BS, OFF, norm)
        if t == 0:
            first = first + jnp.where(pos > 0, 0.0, OFF)
        if t == pairs - 1:
            last = last + jnp.where(pos < GROUP - 1, 0.0, OFF)
        s = dot(k, q, NT) * c2
        w = jnp.concatenate(
            [
                jnp.exp2(s[:BS] - first),
                jnp.exp2(s[BS : 3 * BS] - norm),
                jnp.exp2(s[3 * BS :] - last),
            ],
            axis=0,
        )
        ds = w * (dot(v, g, NT) - rdot)
        wb, dsb = w.astype(jnp.bfloat16), ds.astype(jnp.bfloat16)
        dq_sum[rows, :] += dot(dsb, k, TN)
        dk_sum[span, :] += dot(dsb, q)
        dv_sum[span, :] += dot(wb, g)

    lax.fori_loop(0, (count + BATCH - 1) // BATCH, batch, 0)

    dq_own[...] = dq_sum[pl.ds(0, tokens), :] * SCALE
    for r in range(remote):
        dq_far[r][...] = (dq_sum[pl.ds((r + 1) * tokens, tokens), :] * SCALE).astype(jnp.bfloat16)
    for j in range(GROUP):
        rows = pl.ds(aligned(BS + (pos ^ j) * tokens), tokens)
        for total, keep, send, axis, factor in (
            (dk_sum, dk_keep, dk_send, 1, SCALE),
            (dv_sum, dv_keep, dv_send, 2, 1.0),
        ):
            slot = (j >> 1) if axis == 1 else (j & 1)
            target = send if j & axis else keep
            part = total[rows, :]
            part = part * factor if factor != 1.0 else part
            target[slot] = part.astype(jnp.bfloat16)


def on_device(
    queries, key_states, value_states, forward_out, grad_out, random_blocks, global_blocks
):
    seq_count = lax.axis_size("seq")
    me = lax.axis_index("seq")
    tokens = queries.shape[0]
    blocks = tokens // BS
    heads = queries.shape[1] // DH
    sources = seq_count // GROUP
    remote = sources - 1
    sizes = (seq_count, remote, blocks, heads)

    def shift(array, r):
        pairs = [(i, (i + GROUP * r) % seq_count) for i in range(seq_count)]
        return lax.ppermute(array, "seq", pairs)

    def flip(array, j):
        return lax.ppermute(array, "seq", [(i, i ^ j) for i in range(seq_count)])

    def after(array, other):
        return lax.optimization_barrier((array, other))[0]

    def whole(array, place=None):
        return [(array, place, 0)]

    cuts = [round(heads * x) for x in CUTS]
    chunks = list(zip(cuts[:-1], cuts[1:]))
    k_z = flip(key_states, 2)
    q_all = whole(queries)
    for r in range(1, sources):
        q_all += whole(shift(queries, r))
    kv_x = flip(jnp.stack([key_states, value_states]), 1)
    k_all = whole(key_states) + whole(kv_x, 0) + whole(k_z) + whole(flip(k_z, 1))

    v_chunks, previous = [], k_z
    g_all = whole(grad_out)
    for r in range(1, sources):
        g_all += whole(shift(grad_out, r))
    for c, (low, high) in enumerate(chunks):
        cut = slice(low * DH, high * DH)
        v = after(value_states[:, cut], previous)
        own = [(value_states, None, low), (kv_x, 1, low)]
        if c == 0:
            v_z = flip(v, 2)
            v_all = own + [(v_z, None, 0), (flip(v_z, 1), None, 0)]
            previous = v_z
        else:
            v_z = flip(jnp.stack([v, kv_x[1][:, cut]]), 2)
            v_all = own + [(v_z, 0, 0), (v_z, 1, 0)]
            previous = v_z
        v_chunks.append(v_all)

    meta = jnp.concatenate([me.astype(jnp.int32)[None], global_blocks.astype(jnp.int32)])
    table = random_blocks.reshape(-1)

    def spec(operand, head0):
        _, place, first = operand
        if place is None:
            return pl.BlockSpec((tokens, DH), lambda h, *_: (0, h + head0 + first))
        return pl.BlockSpec((None, tokens, DH), lambda h, *_: (place, 0, h + head0 + first))

    def arrays(operands):
        return [array for array, _, _ in operands]

    padded_rows = (GROUP * tokens + 2 * BS, DH)
    partial_norms = pl.pallas_call(
        partial(norm_kernel, sizes),
        grid_spec=pltpu.PrefetchScalarGridSpec(
            num_scalar_prefetch=2,
            grid=(heads,),
            in_specs=[spec(x, 0) for x in q_all + k_all],
            out_specs=pl.BlockSpec((sources, 1, blocks, BS), lambda h, *_: (0, h, 0, 0)),
            scratch_shapes=[pltpu.VMEM(padded_rows, jnp.bfloat16)],
        ),
        out_shape=jax.ShapeDtypeStruct((sources, heads, blocks, BS), jnp.float32),
        compiler_params=pltpu.CompilerParams(vmem_limit_bytes=48 * 2**20),
        name="partial_norms",
    )(meta, table, *arrays(q_all + k_all))

    row_dot = jnp.sum(
        grad_out.astype(jnp.float32).reshape(tokens, heads, DH)
        * forward_out.astype(jnp.float32).reshape(tokens, heads, DH),
        axis=-1,
    )
    row_dot = row_dot.reshape(blocks, BS, heads).transpose(2, 0, 1)

    mine = jnp.concatenate([partial_norms, row_dot[None]], axis=0)
    told = [mine] + [shift(mine, r) for r in range(1, sources)]
    norms, dots = [], []
    for r in range(sources):
        parts = jnp.stack([told[k][(r - k) % sources] for k in range(sources)])
        top = jnp.max(parts, axis=0)
        norms.append(top + jnp.log2(jnp.sum(jnp.exp2(parts - top), axis=0)))
        dots.append(told[r][sources])
    norms, dots = jnp.stack(norms), jnp.stack(dots)

    def by_item(array):
        array = array.transpose(1, 0, 2, 3).reshape(heads, sources * blocks, BS)
        return jnp.concatenate([array, array], axis=-1)

    def flat(array):
        return array.reshape(sources, heads, 1, tokens)

    def gradients(c):
        head0, count = chunks[c][0], chunks[c][1] - chunks[c][0]
        width = count * DH
        item_spec = pl.BlockSpec((1, sources * blocks, 2 * BS), lambda h, *_: (h + head0, 0, 0))
        flat_spec = pl.BlockSpec((sources, 1, 1, tokens), lambda h, *_: (0, h + head0, 0, 0))
        out_column = pl.BlockSpec((tokens, DH), lambda h, *_: (0, h))
        half_spec = pl.BlockSpec((GROUP // 2, tokens, DH), lambda h, *_: (0, 0, h))
        half_shape = jax.ShapeDtypeStruct((GROUP // 2, tokens, width), jnp.bfloat16)
        return pl.pallas_call(
            partial(grads_kernel, sizes, head0),
            grid_spec=pltpu.PrefetchScalarGridSpec(
                num_scalar_prefetch=2,
                grid=(count,),
                in_specs=[spec(x, head0) for x in q_all]
                + [spec(x, head0) for x in g_all]
                + [spec(x, head0) for x in k_all]
                + [spec(x, 0) for x in v_chunks[c]]
                + [item_spec] * 2
                + [flat_spec] * 2,
                out_specs=[out_column] * sources + [half_spec] * 4,
                scratch_shapes=[
                    pltpu.VMEM((sources * tokens, DH), jnp.bfloat16),
                    pltpu.VMEM((sources * tokens, DH), jnp.bfloat16),
                    pltpu.VMEM(padded_rows, jnp.bfloat16),
                    pltpu.VMEM(padded_rows, jnp.bfloat16),
                    pltpu.VMEM((sources * tokens, DH), jnp.float32),
                    pltpu.VMEM(padded_rows, jnp.float32),
                    pltpu.VMEM(padded_rows, jnp.float32),
                    pltpu.VMEM((BATCH // 2, 2 * BS, 2 * BS), jnp.bfloat16),
                    pltpu.VMEM((BATCH // 2, 2 * BS, 2 * BS), jnp.bfloat16),
                    pltpu.SMEM((2, sources * (3 * blocks + 2) + 2 * BATCH), jnp.int32),
                ],
            ),
            out_shape=[jax.ShapeDtypeStruct((tokens, width), jnp.float32)]
            + [jax.ShapeDtypeStruct((tokens, width), jnp.bfloat16)] * remote
            + [half_shape] * 4,
            compiler_params=pltpu.CompilerParams(vmem_limit_bytes=48 * 2**20),
            name="gradients",
        )(
            meta,
            table,
            *arrays(q_all + g_all + k_all + v_chunks[c]),
            by_item(norms),
            by_item(dots),
            flat(norms),
            flat(dots),
        )

    def wide(array):
        return array.astype(jnp.float32)

    def reduced(keep, send, first, second):
        got = flip(send, first)
        onward = flip((wide(keep[1]) + wide(got[1])).astype(jnp.bfloat16), second)
        return (wide(keep[0]) + wide(got[0]) + wide(onward)).astype(jnp.bfloat16)

    def to_tokens(array):
        return lax.all_to_all(array, "head", split_axis=0, concat_axis=1, tiled=True)

    dq_parts, dk_parts, dv_parts = [], [], []
    for c in range(len(chunks)):
        outs = gradients(c)
        dq, dq_far = outs[0], outs[1:sources]
        dk_keep, dk_send, dv_keep, dv_send = outs[sources:]
        for r in range(1, sources):
            dq = dq + wide(shift(dq_far[r - 1], -r))
        dq_parts.append(dq.astype(jnp.bfloat16))
        dk_parts.append(reduced(dk_keep, dk_send, 1, 2))
        dv_parts.append(reduced(dv_keep, dv_send, 2, 1))
    dq, dk, dv = (
        to_tokens(jnp.concatenate(parts, axis=1)) for parts in (dq_parts, dk_parts, dv_parts)
    )
    return dq, dk, dv


def solution(mesh):
    return jax.shard_map(
        on_device,
        mesh=mesh,
        in_specs=(
            P("seq", "head"),
            P("seq", "head"),
            P("seq", "head"),
            P("seq", "head"),
            P("seq", "head"),
            P(None, "head", None),
            P(),
        ),
        out_specs=(P(("seq", "head"), None), P(("seq", "head"), None), P(("seq", "head"), None)),
        check_vma=False,
    )
```

```python
from functools import partial
import math

import jax
import jax.numpy as jnp
from jax import lax
from jax.experimental import pallas as pl
from jax.experimental.pallas import tpu as pltpu
from jax.sharding import PartitionSpec as P

DH = 128
BS = 64
GROUP = 4
BATCH = 8
CUTS = (0.0, 0.5, 1.0)
JOINED = 4
LOG2E = math.log2(math.e)
SCALE = DH**-0.5
OFF = 1e30
NT = (((1,), (1,)), ((), ()))
TN = (((0,), (0,)), ((), ()))


def dot(a, b, dims=(((1,), (0,)), ((), ()))):
    return lax.dot_general(a, b, dims, preferred_element_type=jnp.float32)


def aligned(start):
    return pl.multiple_of(start, BS)


def place_group(me, key_refs, key_rows, tokens):
    for j, ref in enumerate(key_refs):
        start = aligned(BS + (lax.rem(me, GROUP) ^ j) * tokens)
        key_rows[pl.ds(start, tokens), :] = ref[...]


def zero_ends(key_rows):
    edge = jnp.zeros((BS, DH), key_rows.dtype)
    key_rows[pl.ds(0, BS), :] = edge
    key_rows[pl.ds(key_rows.shape[0] - BS, BS), :] = edge


def local_block(block, group, group_blocks):
    place = block - group * group_blocks
    inside = (place >= 0) & (place < group_blocks)
    return jnp.where(inside, place, 0), inside


def edge_block(src, b, blocks, seq_count, group, group_blocks):
    last = blocks - 1
    if b == 0:
        return local_block(src * blocks - 1, group, group_blocks)
    if b == last:
        return local_block((src + 1) * blocks, group, group_blocks)
    return None


def norm_kernel(sizes, meta, table, *refs):
    seq_count, remote, blocks, heads = sizes
    sources = remote + 1
    tokens = blocks * BS
    q_refs = refs[:sources]
    k_refs = refs[sources : sources + GROUP]
    out_ref, key_rows = refs[sources + GROUP :]
    head = pl.program_id(0)
    me = meta[0]
    group = me // GROUP
    group_blocks = GROUP * blocks
    c2 = SCALE * LOG2E

    @pl.when(head == 0)
    def _():
        zero_ends(key_rows)

    place_group(me, k_refs, key_rows, tokens)
    globs = [local_block(meta[1 + j], group, group_blocks) for j in range(2)]
    glob_keys = [key_rows[pl.ds(aligned(BS + p * BS), BS), :] for p, _ in globs]

    pos = lax.rem(me, GROUP)
    lane = lax.broadcasted_iota(jnp.int32, (1, 2 * BS), 1)
    for r in range(sources):
        src = lax.rem(me - GROUP * r + seq_count, seq_count)
        for t in range(blocks // 2):
            q = q_refs[r][pl.ds(t * 2 * BS, 2 * BS), :]
            tiles, off = [], []
            if r == 0:
                start = aligned((pos * blocks + 2 * t) * BS)
                tiles.append(key_rows[pl.ds(start, 4 * BS), :])
                first = jnp.where(pos > 0, 0.0, OFF) if t == 0 else 0.0
                last = jnp.where(pos < GROUP - 1, 0.0, OFF) if t == blocks // 2 - 1 else 0.0
                off += [(first, OFF), None, None, (OFF, last)]
            for j in range(2):
                tiles.append(glob_keys[j])
                here = jnp.where(globs[j][1], 0.0, OFF)
                off.append((here, here))
            for u in range(2):
                b = 2 * t + u
                found = [
                    local_block(table[((src * blocks + b) * heads + head) * 3 + j], group, group_blocks)
                    for j in range(3)
                ]
                edge = edge_block(src, b, blocks, seq_count, group, group_blocks)
                if r > 0 and edge is not None:
                    found.append(edge)
                for place, inside in found:
                    tiles.append(key_rows[pl.ds(aligned(BS + place * BS), BS), :])
                    here = jnp.where(inside, 0.0, OFF)
                    off.append((here, OFF) if u == 0 else (OFF, here))
            products = dot(jnp.concatenate(tiles, axis=0), q, NT)
            scores = []
            for j, pair in enumerate(off):
                s = products[j * BS : (j + 1) * BS] * c2
                if pair is not None:
                    s = s - jnp.where(lane < BS, pair[0], pair[1])
                scores.append(s)
            top = scores[0]
            for s in scores[1:]:
                top = jnp.maximum(top, s)
            top = jnp.max(top, axis=0, keepdims=True)
            total = jnp.exp2(scores[0] - top)
            for s in scores[1:]:
                total = total + jnp.exp2(s - top)
            found = top + jnp.log2(jnp.sum(total, axis=0, keepdims=True))
            out_ref[r, 0, pl.ds(2 * t, 1), :] = found[:, :BS]
            out_ref[r, 0, pl.ds(2 * t + 1, 1), :] = found[:, BS:]


def grads_kernel(sizes, head0, meta, table, *refs):
    seq_count, remote, blocks, heads = sizes
    sources = remote + 1
    tokens = blocks * BS
    refs = list(refs)

    def take(count):
        taken = refs[:count]
        del refs[:count]
        return taken

    q_refs, g_refs = take(sources), take(sources)
    k_refs, v_refs = take(GROUP), take(GROUP)
    norm_ref, dot_ref, norm_flat, dot_flat = take(4)
    (dq_own,) = take(1)
    dq_far = take(remote)
    dk_keep, dk_send, dv_keep, dv_send = take(4)
    q_rows, g_rows, k_rows, v_rows, dq_sum, dk_sum, dv_sum, w_kept, ds_kept, listed = refs
    head = pl.program_id(0) + head0
    me = meta[0]
    pos = lax.rem(me, GROUP)
    group = me // GROUP
    group_blocks = GROUP * blocks
    c2 = SCALE * LOG2E

    @pl.when(pl.program_id(0) == 0)
    def _():
        zero_ends(k_rows)
        zero_ends(v_rows)

    place_group(me, k_refs, k_rows, tokens)
    place_group(me, v_refs, v_rows, tokens)
    for r in range(sources):
        q_rows[pl.ds(r * tokens, tokens), :] = q_refs[r][...]
        g_rows[pl.ds(r * tokens, tokens), :] = g_refs[r][...]
    dk_sum[...] = jnp.zeros_like(dk_sum)
    dv_sum[...] = jnp.zeros_like(dv_sum)
    dq_sum[...] = jnp.zeros_like(dq_sum)

    count = jnp.int32(0)

    def note(count, item, place, inside):
        listed[0, count] = item
        listed[1, count] = place
        return count + inside.astype(jnp.int32)

    for r in range(sources):
        src = lax.rem(me - GROUP * r + seq_count, seq_count)
        for b in range(blocks):
            item = r * blocks + b
            for j in range(3):
                entry = table[((src * blocks + b) * heads + head) * 3 + j]
                count = note(count, item, *local_block(entry, group, group_blocks))
            if r > 0:
                found = edge_block(src, b, blocks, seq_count, group, group_blocks)
                if found is not None:
                    count = note(count, item, *found)
    for u in range(2 * BATCH):
        listed[0, count + u] = 0
        listed[1, count + u] = 0

    lane = lax.broadcasted_iota(jnp.int32, (1, 2 * BS), 1)

    globs = [local_block(meta[1 + j], group, group_blocks) for j in range(2)]
    wide = tokens

    spans = [pl.ds(aligned(BS + p * BS), BS) for p, _ in globs]
    k = jnp.concatenate([k_rows[s, :] for s in spans], axis=0)
    v = jnp.concatenate([v_rows[s, :] for s in spans], axis=0)
    off = [jnp.where(inside, 0.0, OFF) for _, inside in globs]
    dk = jnp.zeros((2 * BS, DH), jnp.float32)
    dv = jnp.zeros((2 * BS, DH), jnp.float32)
    for r in range(sources):
        for t in range(tokens // wide):
            rows = pl.ds(r * tokens + t * wide, wide)
            q, g = q_rows[rows, :], g_rows[rows, :]
            norm = norm_flat[r, 0, :, t * wide : (t + 1) * wide]
            rdot = dot_flat[r, 0, :, t * wide : (t + 1) * wide]
            s = dot(k, q, NT) * c2
            w = jnp.concatenate(
                [jnp.exp2(s[:BS] - (norm + off[0])), jnp.exp2(s[BS:] - (norm + off[1]))],
                axis=0,
            )
            ds = w * (dot(v, g, NT) - rdot)
            wb, dsb = w.astype(jnp.bfloat16), ds.astype(jnp.bfloat16)
            dq_sum[rows, :] += dot(dsb, k, TN)
            dk = dk + dot(dsb, q)
            dv = dv + dot(wb, g)
    for j, span in enumerate(spans):
        dk_sum[span, :] += dk[j * BS : (j + 1) * BS]
        dv_sum[span, :] += dv[j * BS : (j + 1) * BS]

    def places(step):
        rows, spans = [], []
        for u in range(BATCH):
            rows.append(pl.ds(aligned(listed[0, step * BATCH + u] * BS), BS))
            spans.append(pl.ds(aligned(BS + listed[1, step * BATCH + u] * BS), BS))
        return rows, spans

    def joined(ref, slices):
        return jnp.concatenate([ref[x, :] for x in slices], axis=0)

    def weigh(step):
        rows, spans = places(step)
        weighed = []
        for first in range(0, BATCH, JOINED):
            these = slice(first, first + JOINED)
            s = dot(joined(k_rows, spans[these]), joined(q_rows, rows[these]), NT)
            dw = dot(joined(v_rows, spans[these]), joined(g_rows, rows[these]), NT)
            for t in range(JOINED // 2):
                norms, dots = [], []
                for u in (first + 2 * t, first + 2 * t + 1):
                    item = listed[0, step * BATCH + u]
                    off = jnp.where(step * BATCH + u < count, 0.0, OFF)
                    norms.append(norm_ref[0, pl.ds(item, 1), :] + off)
                    dots.append(dot_ref[0, pl.ds(item, 1), :])
                part = slice(t * 2 * BS, (t + 1) * 2 * BS)
                both = s[part, part] * c2
                w = jnp.concatenate(
                    [
                        jnp.exp2(both[:BS] - jnp.where(lane < BS, norms[0], OFF)),
                        jnp.exp2(both[BS:] - jnp.where(lane < BS, OFF, norms[1])),
                    ],
                    axis=0,
                )
                ds = w * (dw[part, part] - jnp.where(lane < BS, dots[0], dots[1]))
                weighed.append((w.astype(jnp.bfloat16), ds.astype(jnp.bfloat16)))
        return weighed

    def keep_weighed(weighed):
        for t, (w, ds) in enumerate(weighed):
            w_kept[t], ds_kept[t] = w, ds

    def batch(step, carry):
        held = [(w_kept[t], ds_kept[t]) for t in range(BATCH // 2)]
        following = weigh(step + 1)
        rows, spans = places(step)
        done = []
        for t, (wb, dsb) in enumerate(held):
            pair = slice(2 * t, 2 * t + 2)
            q, g, k = joined(q_rows, rows[pair]), joined(g_rows, rows[pair]), joined(k_rows, spans[pair])
            done.append((dot(dsb, k, TN), dot(dsb, q), dot(wb, g)))
        keep_weighed(following)
        for u in range(BATCH):
            dq, dk, dv = done[u // 2]
            part = slice((u % 2) * BS, (u % 2 + 1) * BS)
            dq_sum[rows[u], :] += dq[part]
            dk_sum[spans[u], :] += dk[part]
            dv_sum[spans[u], :] += dv[part]
        return carry

    keep_weighed(weigh(0))
    pairs = blocks // 2
    for t in range(pairs):
        rows = pl.ds(t * 2 * BS, 2 * BS)
        q, g = q_refs[0][rows, :], g_refs[0][rows, :]
        start = aligned((pos * blocks + 2 * t) * BS)
        span = pl.ds(start, 4 * BS)
        k, v = k_rows[span, :], v_rows[span, :]
        norm = norm_flat[0, 0, :, t * 2 * BS : (t + 1) * 2 * BS]
        rdot = dot_flat[0, 0, :, t * 2 * BS : (t + 1) * 2 * BS]
        first = jnp.where(lane < BS, norm, OFF)
        last = jnp.where(lane < BS, OFF, norm)
        if t == 0:
            first = first + jnp.where(pos > 0, 0.0, OFF)
        if t == pairs - 1:
            last = last + jnp.where(pos < GROUP - 1, 0.0, OFF)
        s = dot(k, q, NT) * c2
        w = jnp.concatenate(
            [
                jnp.exp2(s[:BS] - first),
                jnp.exp2(s[BS : 3 * BS] - norm),
                jnp.exp2(s[3 * BS :] - last),
            ],
            axis=0,
        )
        ds = w * (dot(v, g, NT) - rdot)
        wb, dsb = w.astype(jnp.bfloat16), ds.astype(jnp.bfloat16)
        dq_sum[rows, :] += dot(dsb, k, TN)
        dk_sum[span, :] += dot(dsb, q)
        dv_sum[span, :] += dot(wb, g)

    lax.fori_loop(0, (count + BATCH - 1) // BATCH, batch, 0)

    dq_own[...] = dq_sum[pl.ds(0, tokens), :] * SCALE
    for r in range(remote):
        dq_far[r][...] = (dq_sum[pl.ds((r + 1) * tokens, tokens), :] * SCALE).astype(jnp.bfloat16)
    for j in range(GROUP):
        rows = pl.ds(aligned(BS + (pos ^ j) * tokens), tokens)
        for total, keep, send, axis, factor in (
            (dk_sum, dk_keep, dk_send, 1, SCALE),
            (dv_sum, dv_keep, dv_send, 2, 1.0),
        ):
            slot = (j >> 1) if axis == 1 else (j & 1)
            target = send if j & axis else keep
            part = total[rows, :]
            part = part * factor if factor != 1.0 else part
            target[slot] = part.astype(jnp.bfloat16)


def on_device(
    queries, key_states, value_states, forward_out, grad_out, random_blocks, global_blocks
):
    seq_count = lax.axis_size("seq")
    me = lax.axis_index("seq")
    tokens = queries.shape[0]
    blocks = tokens // BS
    heads = queries.shape[1] // DH
    sources = seq_count // GROUP
    remote = sources - 1
    sizes = (seq_count, remote, blocks, heads)

    def shift(array, r):
        pairs = [(i, (i + GROUP * r) % seq_count) for i in range(seq_count)]
        return lax.ppermute(array, "seq", pairs)

    def flip(array, j):
        return lax.ppermute(array, "seq", [(i, i ^ j) for i in range(seq_count)])

    def after(array, other):
        return lax.optimization_barrier((array, other))[0]

    def whole(array, place=None):
        return [(array, place, 0)]

    cuts = [round(heads * x) for x in CUTS]
    chunks = list(zip(cuts[:-1], cuts[1:]))
    k_z = flip(key_states, 2)
    q_all = whole(queries)
    for r in range(1, sources):
        q_all += whole(shift(queries, r))
    kv_x = flip(jnp.stack([key_states, value_states]), 1)
    k_all = whole(key_states) + whole(kv_x, 0) + whole(k_z) + whole(flip(k_z, 1))

    v_chunks, previous = [], k_z
    g_all = whole(grad_out)
    for r in range(1, sources):
        g_all += whole(shift(grad_out, r))
    for c, (low, high) in enumerate(chunks):
        cut = slice(low * DH, high * DH)
        v = after(value_states[:, cut], previous)
        own = [(value_states, None, low), (kv_x, 1, low)]
        if c == 0:
            v_z = flip(v, 2)
            v_all = own + [(v_z, None, 0), (flip(v_z, 1), None, 0)]
            previous = v_z
        else:
            v_z = flip(jnp.stack([v, kv_x[1][:, cut]]), 2)
            v_all = own + [(v_z, 0, 0), (v_z, 1, 0)]
            previous = v_z
        v_chunks.append(v_all)

    meta = jnp.concatenate([me.astype(jnp.int32)[None], global_blocks.astype(jnp.int32)])
    table = random_blocks.reshape(-1)

    def spec(operand, head0):
        _, place, first = operand
        if place is None:
            return pl.BlockSpec((tokens, DH), lambda h, *_: (0, h + head0 + first))
        return pl.BlockSpec((None, tokens, DH), lambda h, *_: (place, 0, h + head0 + first))

    def arrays(operands):
        return [array for array, _, _ in operands]

    padded_rows = (GROUP * tokens + 2 * BS, DH)
    partial_norms = pl.pallas_call(
        partial(norm_kernel, sizes),
        grid_spec=pltpu.PrefetchScalarGridSpec(
            num_scalar_prefetch=2,
            grid=(heads,),
            in_specs=[spec(x, 0) for x in q_all + k_all],
            out_specs=pl.BlockSpec((sources, 1, blocks, BS), lambda h, *_: (0, h, 0, 0)),
            scratch_shapes=[pltpu.VMEM(padded_rows, jnp.bfloat16)],
        ),
        out_shape=jax.ShapeDtypeStruct((sources, heads, blocks, BS), jnp.float32),
        compiler_params=pltpu.CompilerParams(vmem_limit_bytes=48 * 2**20),
        name="partial_norms",
    )(meta, table, *arrays(q_all + k_all))

    row_dot = jnp.sum(
        grad_out.astype(jnp.float32).reshape(tokens, heads, DH)
        * forward_out.astype(jnp.float32).reshape(tokens, heads, DH),
        axis=-1,
    )
    row_dot = row_dot.reshape(blocks, BS, heads).transpose(2, 0, 1)

    mine = jnp.concatenate([partial_norms, row_dot[None]], axis=0)
    told = [mine] + [shift(mine, r) for r in range(1, sources)]
    norms, dots = [], []
    for r in range(sources):
        parts = jnp.stack([told[k][(r - k) % sources] for k in range(sources)])
        top = jnp.max(parts, axis=0)
        norms.append(top + jnp.log2(jnp.sum(jnp.exp2(parts - top), axis=0)))
        dots.append(told[r][sources])
    norms, dots = jnp.stack(norms), jnp.stack(dots)

    def by_item(array):
        array = array.transpose(1, 0, 2, 3).reshape(heads, sources * blocks, BS)
        return jnp.concatenate([array, array], axis=-1)

    def flat(array):
        return array.reshape(sources, heads, 1, tokens)

    def gradients(c):
        head0, count = chunks[c][0], chunks[c][1] - chunks[c][0]
        width = count * DH
        item_spec = pl.BlockSpec((1, sources * blocks, 2 * BS), lambda h, *_: (h + head0, 0, 0))
        flat_spec = pl.BlockSpec((sources, 1, 1, tokens), lambda h, *_: (0, h + head0, 0, 0))
        out_column = pl.BlockSpec((tokens, DH), lambda h, *_: (0, h))
        half_spec = pl.BlockSpec((GROUP // 2, tokens, DH), lambda h, *_: (0, 0, h))
        half_shape = jax.ShapeDtypeStruct((GROUP // 2, tokens, width), jnp.bfloat16)
        return pl.pallas_call(
            partial(grads_kernel, sizes, head0),
            grid_spec=pltpu.PrefetchScalarGridSpec(
                num_scalar_prefetch=2,
                grid=(count,),
                in_specs=[spec(x, head0) for x in q_all]
                + [spec(x, head0) for x in g_all]
                + [spec(x, head0) for x in k_all]
                + [spec(x, 0) for x in v_chunks[c]]
                + [item_spec] * 2
                + [flat_spec] * 2,
                out_specs=[out_column] * sources + [half_spec] * 4,
                scratch_shapes=[
                    pltpu.VMEM((sources * tokens, DH), jnp.bfloat16),
                    pltpu.VMEM((sources * tokens, DH), jnp.bfloat16),
                    pltpu.VMEM(padded_rows, jnp.bfloat16),
                    pltpu.VMEM(padded_rows, jnp.bfloat16),
                    pltpu.VMEM((sources * tokens, DH), jnp.float32),
                    pltpu.VMEM(padded_rows, jnp.float32),
                    pltpu.VMEM(padded_rows, jnp.float32),
                    pltpu.VMEM((BATCH // 2, 2 * BS, 2 * BS), jnp.bfloat16),
                    pltpu.VMEM((BATCH // 2, 2 * BS, 2 * BS), jnp.bfloat16),
                    pltpu.SMEM((2, sources * (3 * blocks + 2) + 2 * BATCH), jnp.int32),
                ],
            ),
            out_shape=[jax.ShapeDtypeStruct((tokens, width), jnp.float32)]
            + [jax.ShapeDtypeStruct((tokens, width), jnp.bfloat16)] * remote
            + [half_shape] * 4,
            compiler_params=pltpu.CompilerParams(vmem_limit_bytes=48 * 2**20),
            name="gradients",
        )(
            meta,
            table,
            *arrays(q_all + g_all + k_all + v_chunks[c]),
            by_item(norms),
            by_item(dots),
            flat(norms),
            flat(dots),
        )

    def wide(array):
        return array.astype(jnp.float32)

    def reduced(keep, send, first, second):
        got = flip(send, first)
        onward = flip((wide(keep[1]) + wide(got[1])).astype(jnp.bfloat16), second)
        return (wide(keep[0]) + wide(got[0]) + wide(onward)).astype(jnp.bfloat16)

    def to_tokens(array):
        return lax.all_to_all(array, "head", split_axis=0, concat_axis=1, tiled=True)

    dq_parts, dk_parts, dv_parts = [], [], []
    for c in range(len(chunks)):
        outs = gradients(c)
        dq, dq_far = outs[0], outs[1:sources]
        dk_keep, dk_send, dv_keep, dv_send = outs[sources:]
        for r in range(1, sources):
            dq = dq + wide(shift(dq_far[r - 1], -r))
        dq_parts.append(dq.astype(jnp.bfloat16))
        dk_parts.append(reduced(dk_keep, dk_send, 1, 2))
        dv_parts.append(reduced(dv_keep, dv_send, 2, 1))
    def to_tokens_by_steps(array):
        groups = lax.axis_size("head")
        here = lax.axis_index("head")
        rows = array.reshape(groups, tokens // groups, -1)

        def row(stack, index):
            return lax.dynamic_index_in_dim(stack, lax.rem(index, groups), 0, keepdims=False)

        got = [row(rows, here)]
        for m in range(1, groups):
            pairs = [(i, (i + m) % groups) for i in range(groups)]
            got.append(lax.ppermute(row(rows, here + m), "head", pairs))
        got = jnp.stack(got)
        return jnp.concatenate([row(got, here + groups - j) for j in range(groups)], axis=1)

    dq = to_tokens_by_steps(jnp.concatenate(dq_parts, axis=1))
    dk = to_tokens(jnp.concatenate(dk_parts, axis=1))
    dv = to_tokens(jnp.concatenate(dv_parts, axis=1))
    return dq, dk, dv


def solution(mesh):
    return jax.shard_map(
        on_device,
        mesh=mesh,
        in_specs=(
            P("seq", "head"),
            P("seq", "head"),
            P("seq", "head"),
            P("seq", "head"),
            P("seq", "head"),
            P(None, "head", None),
            P(),
        ),
        out_specs=(P(("seq", "head"), None), P(("seq", "head"), None), P(("seq", "head"), None)),
        check_vma=False,
    )
```

```python
from functools import partial
import math

import jax
import jax.numpy as jnp
from jax import lax
from jax.experimental import pallas as pl
from jax.experimental.pallas import tpu as pltpu
from jax.sharding import PartitionSpec as P

DH = 128
BS = 64
GROUP = 4
BATCH = 8
CUTS = (0.0, 0.5, 1.0)
VALUE_AXES = (1, 2)
JOINED = 4
LOG2E = math.log2(math.e)
SCALE = DH**-0.5
OFF = 1e30
NT = (((1,), (1,)), ((), ()))
TN = (((0,), (0,)), ((), ()))


def dot(a, b, dims=(((1,), (0,)), ((), ()))):
    return lax.dot_general(a, b, dims, preferred_element_type=jnp.float32)


def aligned(start):
    return pl.multiple_of(start, BS)


def place_group(me, key_refs, key_rows, tokens):
    for j, ref in enumerate(key_refs):
        start = aligned(BS + (lax.rem(me, GROUP) ^ j) * tokens)
        key_rows[pl.ds(start, tokens), :] = ref[...]


def zero_ends(key_rows):
    edge = jnp.zeros((BS, DH), key_rows.dtype)
    key_rows[pl.ds(0, BS), :] = edge
    key_rows[pl.ds(key_rows.shape[0] - BS, BS), :] = edge


def local_block(block, group, group_blocks):
    place = block - group * group_blocks
    inside = (place >= 0) & (place < group_blocks)
    return jnp.where(inside, place, 0), inside


def edge_block(src, b, blocks, seq_count, group, group_blocks):
    last = blocks - 1
    if b == 0:
        return local_block(src * blocks - 1, group, group_blocks)
    if b == last:
        return local_block((src + 1) * blocks, group, group_blocks)
    return None


def norm_kernel(sizes, meta, table, *refs):
    seq_count, remote, blocks, heads = sizes
    sources = remote + 1
    tokens = blocks * BS
    q_refs = refs[:sources]
    k_refs = refs[sources : sources + GROUP]
    out_ref, key_rows = refs[sources + GROUP :]
    head = pl.program_id(0)
    me = meta[0]
    group = me // GROUP
    group_blocks = GROUP * blocks
    c2 = SCALE * LOG2E

    @pl.when(head == 0)
    def _():
        zero_ends(key_rows)

    place_group(me, k_refs, key_rows, tokens)
    globs = [local_block(meta[1 + j], group, group_blocks) for j in range(2)]
    glob_keys = [key_rows[pl.ds(aligned(BS + p * BS), BS), :] for p, _ in globs]

    pos = lax.rem(me, GROUP)
    lane = lax.broadcasted_iota(jnp.int32, (1, 2 * BS), 1)
    for r in range(sources):
        src = lax.rem(me - GROUP * r + seq_count, seq_count)
        for t in range(blocks // 2):
            q = q_refs[r][pl.ds(t * 2 * BS, 2 * BS), :]
            tiles, off = [], []
            if r == 0:
                start = aligned((pos * blocks + 2 * t) * BS)
                tiles.append(key_rows[pl.ds(start, 4 * BS), :])
                first = jnp.where(pos > 0, 0.0, OFF) if t == 0 else 0.0
                last = jnp.where(pos < GROUP - 1, 0.0, OFF) if t == blocks // 2 - 1 else 0.0
                off += [(first, OFF), None, None, (OFF, last)]
            for j in range(2):
                tiles.append(glob_keys[j])
                here = jnp.where(globs[j][1], 0.0, OFF)
                off.append((here, here))
            for u in range(2):
                b = 2 * t + u
                found = [
                    local_block(table[((src * blocks + b) * heads + head) * 3 + j], group, group_blocks)
                    for j in range(3)
                ]
                edge = edge_block(src, b, blocks, seq_count, group, group_blocks)
                if r > 0 and edge is not None:
                    found.append(edge)
                for place, inside in found:
                    tiles.append(key_rows[pl.ds(aligned(BS + place * BS), BS), :])
                    here = jnp.where(inside, 0.0, OFF)
                    off.append((here, OFF) if u == 0 else (OFF, here))
            products = dot(jnp.concatenate(tiles, axis=0), q, NT)
            scores = []
            for j, pair in enumerate(off):
                s = products[j * BS : (j + 1) * BS] * c2
                if pair is not None:
                    s = s - jnp.where(lane < BS, pair[0], pair[1])
                scores.append(s)
            top = scores[0]
            for s in scores[1:]:
                top = jnp.maximum(top, s)
            top = jnp.max(top, axis=0, keepdims=True)
            total = jnp.exp2(scores[0] - top)
            for s in scores[1:]:
                total = total + jnp.exp2(s - top)
            found = top + jnp.log2(jnp.sum(total, axis=0, keepdims=True))
            out_ref[r, 0, pl.ds(2 * t, 1), :] = found[:, :BS]
            out_ref[r, 0, pl.ds(2 * t + 1, 1), :] = found[:, BS:]


def grads_kernel(sizes, value_axis, head0, meta, table, *refs):
    seq_count, remote, blocks, heads = sizes
    sources = remote + 1
    tokens = blocks * BS
    refs = list(refs)

    def take(count):
        taken = refs[:count]
        del refs[:count]
        return taken

    q_refs, g_refs = take(sources), take(sources)
    k_refs, v_refs = take(GROUP), take(GROUP)
    norm_ref, dot_ref, norm_flat, dot_flat = take(4)
    (dq_own,) = take(1)
    dq_far = take(remote)
    dk_keep, dk_send, dv_keep, dv_send = take(4)
    q_rows, g_rows, k_rows, v_rows, dq_sum, dk_sum, dv_sum, w_kept, ds_kept, listed = refs
    head = pl.program_id(0) + head0
    me = meta[0]
    pos = lax.rem(me, GROUP)
    group = me // GROUP
    group_blocks = GROUP * blocks
    c2 = SCALE * LOG2E

    @pl.when(pl.program_id(0) == 0)
    def _():
        zero_ends(k_rows)
        zero_ends(v_rows)

    place_group(me, k_refs, k_rows, tokens)
    place_group(me, v_refs, v_rows, tokens)
    for r in range(sources):
        q_rows[pl.ds(r * tokens, tokens), :] = q_refs[r][...]
        g_rows[pl.ds(r * tokens, tokens), :] = g_refs[r][...]
    dk_sum[...] = jnp.zeros_like(dk_sum)
    dv_sum[...] = jnp.zeros_like(dv_sum)
    dq_sum[...] = jnp.zeros_like(dq_sum)

    count = jnp.int32(0)

    def note(count, item, place, inside):
        listed[0, count] = item
        listed[1, count] = place
        return count + inside.astype(jnp.int32)

    for r in range(sources):
        src = lax.rem(me - GROUP * r + seq_count, seq_count)
        for b in range(blocks):
            item = r * blocks + b
            for j in range(3):
                entry = table[((src * blocks + b) * heads + head) * 3 + j]
                count = note(count, item, *local_block(entry, group, group_blocks))
            if r > 0:
                found = edge_block(src, b, blocks, seq_count, group, group_blocks)
                if found is not None:
                    count = note(count, item, *found)
    for u in range(2 * BATCH):
        listed[0, count + u] = 0
        listed[1, count + u] = 0

    lane = lax.broadcasted_iota(jnp.int32, (1, 2 * BS), 1)

    globs = [local_block(meta[1 + j], group, group_blocks) for j in range(2)]
    wide = tokens

    spans = [pl.ds(aligned(BS + p * BS), BS) for p, _ in globs]
    k = jnp.concatenate([k_rows[s, :] for s in spans], axis=0)
    v = jnp.concatenate([v_rows[s, :] for s in spans], axis=0)
    off = [jnp.where(inside, 0.0, OFF) for _, inside in globs]
    dk = jnp.zeros((2 * BS, DH), jnp.float32)
    dv = jnp.zeros((2 * BS, DH), jnp.float32)
    for r in range(sources):
        for t in range(tokens // wide):
            rows = pl.ds(r * tokens + t * wide, wide)
            q, g = q_rows[rows, :], g_rows[rows, :]
            norm = norm_flat[r, 0, :, t * wide : (t + 1) * wide]
            rdot = dot_flat[r, 0, :, t * wide : (t + 1) * wide]
            s = dot(k, q, NT) * c2
            w = jnp.concatenate(
                [jnp.exp2(s[:BS] - (norm + off[0])), jnp.exp2(s[BS:] - (norm + off[1]))],
                axis=0,
            )
            ds = w * (dot(v, g, NT) - rdot)
            wb, dsb = w.astype(jnp.bfloat16), ds.astype(jnp.bfloat16)
            dq_sum[rows, :] += dot(dsb, k, TN)
            dk = dk + dot(dsb, q)
            dv = dv + dot(wb, g)
    for j, span in enumerate(spans):
        dk_sum[span, :] += dk[j * BS : (j + 1) * BS]
        dv_sum[span, :] += dv[j * BS : (j + 1) * BS]

    def places(step):
        rows, spans = [], []
        for u in range(BATCH):
            rows.append(pl.ds(aligned(listed[0, step * BATCH + u] * BS), BS))
            spans.append(pl.ds(aligned(BS + listed[1, step * BATCH + u] * BS), BS))
        return rows, spans

    def joined(ref, slices):
        return jnp.concatenate([ref[x, :] for x in slices], axis=0)

    def weigh(step):
        rows, spans = places(step)
        weighed = []
        for first in range(0, BATCH, JOINED):
            these = slice(first, first + JOINED)
            s = dot(joined(k_rows, spans[these]), joined(q_rows, rows[these]), NT)
            dw = dot(joined(v_rows, spans[these]), joined(g_rows, rows[these]), NT)
            for t in range(JOINED // 2):
                norms, dots = [], []
                for u in (first + 2 * t, first + 2 * t + 1):
                    item = listed[0, step * BATCH + u]
                    off = jnp.where(step * BATCH + u < count, 0.0, OFF)
                    norms.append(norm_ref[0, pl.ds(item, 1), :] + off)
                    dots.append(dot_ref[0, pl.ds(item, 1), :])
                part = slice(t * 2 * BS, (t + 1) * 2 * BS)
                both = s[part, part] * c2
                w = jnp.concatenate(
                    [
                        jnp.exp2(both[:BS] - jnp.where(lane < BS, norms[0], OFF)),
                        jnp.exp2(both[BS:] - jnp.where(lane < BS, OFF, norms[1])),
                    ],
                    axis=0,
                )
                ds = w * (dw[part, part] - jnp.where(lane < BS, dots[0], dots[1]))
                weighed.append((w.astype(jnp.bfloat16), ds.astype(jnp.bfloat16)))
        return weighed

    def keep_weighed(weighed):
        for t, (w, ds) in enumerate(weighed):
            w_kept[t], ds_kept[t] = w, ds

    def batch(step, carry):
        held = [(w_kept[t], ds_kept[t]) for t in range(BATCH // 2)]
        following = weigh(step + 1)
        rows, spans = places(step)
        done = []
        for t, (wb, dsb) in enumerate(held):
            pair = slice(2 * t, 2 * t + 2)
            q, g, k = joined(q_rows, rows[pair]), joined(g_rows, rows[pair]), joined(k_rows, spans[pair])
            done.append((dot(dsb, k, TN), dot(dsb, q), dot(wb, g)))
        keep_weighed(following)
        for u in range(BATCH):
            dq, dk, dv = done[u // 2]
            part = slice((u % 2) * BS, (u % 2 + 1) * BS)
            dq_sum[rows[u], :] += dq[part]
            dk_sum[spans[u], :] += dk[part]
            dv_sum[spans[u], :] += dv[part]
        return carry

    keep_weighed(weigh(0))
    pairs = blocks // 2
    for t in range(pairs):
        rows = pl.ds(t * 2 * BS, 2 * BS)
        q, g = q_refs[0][rows, :], g_refs[0][rows, :]
        start = aligned((pos * blocks + 2 * t) * BS)
        span = pl.ds(start, 4 * BS)
        k, v = k_rows[span, :], v_rows[span, :]
        norm = norm_flat[0, 0, :, t * 2 * BS : (t + 1) * 2 * BS]
        rdot = dot_flat[0, 0, :, t * 2 * BS : (t + 1) * 2 * BS]
        first = jnp.where(lane < BS, norm, OFF)
        last = jnp.where(lane < BS, OFF, norm)
        if t == 0:
            first = first + jnp.where(pos > 0, 0.0, OFF)
        if t == pairs - 1:
            last = last + jnp.where(pos < GROUP - 1, 0.0, OFF)
        s = dot(k, q, NT) * c2
        w = jnp.concatenate(
            [
                jnp.exp2(s[:BS] - first),
                jnp.exp2(s[BS : 3 * BS] - norm),
                jnp.exp2(s[3 * BS :] - last),
            ],
            axis=0,
        )
        ds = w * (dot(v, g, NT) - rdot)
        wb, dsb = w.astype(jnp.bfloat16), ds.astype(jnp.bfloat16)
        dq_sum[rows, :] += dot(dsb, k, TN)
        dk_sum[span, :] += dot(dsb, q)
        dv_sum[span, :] += dot(wb, g)

    lax.fori_loop(0, (count + BATCH - 1) // BATCH, batch, 0)

    dq_own[...] = (dq_sum[pl.ds(0, tokens), :] * SCALE).astype(jnp.bfloat16)
    for r in range(remote):
        dq_far[r][...] = (dq_sum[pl.ds((r + 1) * tokens, tokens), :] * SCALE).astype(jnp.bfloat16)
    for j in range(GROUP):
        rows = pl.ds(aligned(BS + (pos ^ j) * tokens), tokens)
        for total, keep, send, axis, factor in (
            (dk_sum, dk_keep, dk_send, 1, SCALE),
            (dv_sum, dv_keep, dv_send, value_axis, 1.0),
        ):
            slot = (j >> 1) if axis == 1 else (j & 1)
            target = send if j & axis else keep
            part = total[rows, :]
            part = part * factor if factor != 1.0 else part
            target[slot] = part.astype(jnp.bfloat16)


def on_device(
    queries, key_states, value_states, forward_out, grad_out, random_blocks, global_blocks
):
    seq_count = lax.axis_size("seq")
    me = lax.axis_index("seq")
    tokens = queries.shape[0]
    blocks = tokens // BS
    heads = queries.shape[1] // DH
    sources = seq_count // GROUP
    remote = sources - 1
    sizes = (seq_count, remote, blocks, heads)

    def shift(array, r):
        pairs = [(i, (i + GROUP * r) % seq_count) for i in range(seq_count)]
        return lax.ppermute(array, "seq", pairs)

    def flip(array, j):
        return lax.ppermute(array, "seq", [(i, i ^ j) for i in range(seq_count)])

    def after(array, other):
        return lax.optimization_barrier((array, other))[0]

    def whole(array, place=None):
        return [(array, place, 0)]

    cuts = [round(heads * x) for x in CUTS]
    chunks = list(zip(cuts[:-1], cuts[1:]))
    k_z = flip(key_states, 2)
    q_all = whole(queries)
    for r in range(1, sources):
        q_all += whole(shift(queries, r))
    kv_x = flip(jnp.stack([key_states, value_states]), 1)
    k_all = whole(key_states) + whole(kv_x, 0) + whole(k_z) + whole(flip(k_z, 1))

    v_chunks, previous = [], k_z
    g_all = whole(grad_out)
    for r in range(1, sources):
        g_all += whole(shift(grad_out, r))
    for c, (low, high) in enumerate(chunks):
        cut = slice(low * DH, high * DH)
        v = after(value_states[:, cut], previous)
        own = [(value_states, None, low), (kv_x, 1, low)]
        if c == 0:
            v_z = flip(v, 2)
            v_all = own + [(v_z, None, 0), (flip(v_z, 1), None, 0)]
            previous = v_z
        else:
            v_z = flip(jnp.stack([v, kv_x[1][:, cut]]), 2)
            v_all = own + [(v_z, 0, 0), (v_z, 1, 0)]
            previous = v_z
        v_chunks.append(v_all)

    meta = jnp.concatenate([me.astype(jnp.int32)[None], global_blocks.astype(jnp.int32)])
    table = random_blocks.reshape(-1)

    def spec(operand, head0):
        _, place, first = operand
        if place is None:
            return pl.BlockSpec((tokens, DH), lambda h, *_: (0, h + head0 + first))
        return pl.BlockSpec((None, tokens, DH), lambda h, *_: (place, 0, h + head0 + first))

    def arrays(operands):
        return [array for array, _, _ in operands]

    padded_rows = (GROUP * tokens + 2 * BS, DH)
    partial_norms = pl.pallas_call(
        partial(norm_kernel, sizes),
        grid_spec=pltpu.PrefetchScalarGridSpec(
            num_scalar_prefetch=2,
            grid=(heads,),
            in_specs=[spec(x, 0) for x in q_all + k_all],
            out_specs=pl.BlockSpec((sources, 1, blocks, BS), lambda h, *_: (0, h, 0, 0)),
            scratch_shapes=[pltpu.VMEM(padded_rows, jnp.bfloat16)],
        ),
        out_shape=jax.ShapeDtypeStruct((sources, heads, blocks, BS), jnp.float32),
        compiler_params=pltpu.CompilerParams(vmem_limit_bytes=48 * 2**20),
        name="partial_norms",
    )(meta, table, *arrays(q_all + k_all))

    row_dot = jnp.sum(
        grad_out.astype(jnp.float32).reshape(tokens, heads, DH)
        * forward_out.astype(jnp.float32).reshape(tokens, heads, DH),
        axis=-1,
    )
    row_dot = row_dot.reshape(blocks, BS, heads).transpose(2, 0, 1)

    mine = jnp.concatenate([partial_norms, row_dot[None]], axis=0)
    told = [mine] + [shift(mine, r) for r in range(1, sources)]
    norms, dots = [], []
    for r in range(sources):
        parts = jnp.stack([told[k][(r - k) % sources] for k in range(sources)])
        top = jnp.max(parts, axis=0)
        norms.append(top + jnp.log2(jnp.sum(jnp.exp2(parts - top), axis=0)))
        dots.append(told[r][sources])
    norms, dots = jnp.stack(norms), jnp.stack(dots)

    def by_item(array):
        array = array.transpose(1, 0, 2, 3).reshape(heads, sources * blocks, BS)
        return jnp.concatenate([array, array], axis=-1)

    def flat(array):
        return array.reshape(sources, heads, 1, tokens)

    def gradients(c):
        head0, count = chunks[c][0], chunks[c][1] - chunks[c][0]
        width = count * DH
        item_spec = pl.BlockSpec((1, sources * blocks, 2 * BS), lambda h, *_: (h + head0, 0, 0))
        flat_spec = pl.BlockSpec((sources, 1, 1, tokens), lambda h, *_: (0, h + head0, 0, 0))
        out_column = pl.BlockSpec((tokens, DH), lambda h, *_: (0, h))
        half_spec = pl.BlockSpec((GROUP // 2, tokens, DH), lambda h, *_: (0, 0, h))
        half_shape = jax.ShapeDtypeStruct((GROUP // 2, tokens, width), jnp.bfloat16)
        return pl.pallas_call(
            partial(grads_kernel, sizes, VALUE_AXES[c], head0),
            grid_spec=pltpu.PrefetchScalarGridSpec(
                num_scalar_prefetch=2,
                grid=(count,),
                in_specs=[spec(x, head0) for x in q_all]
                + [spec(x, head0) for x in g_all]
                + [spec(x, head0) for x in k_all]
                + [spec(x, 0) for x in v_chunks[c]]
                + [item_spec] * 2
                + [flat_spec] * 2,
                out_specs=[out_column] * sources + [half_spec] * 4,
                scratch_shapes=[
                    pltpu.VMEM((sources * tokens, DH), jnp.bfloat16),
                    pltpu.VMEM((sources * tokens, DH), jnp.bfloat16),
                    pltpu.VMEM(padded_rows, jnp.bfloat16),
                    pltpu.VMEM(padded_rows, jnp.bfloat16),
                    pltpu.VMEM((sources * tokens, DH), jnp.float32),
                    pltpu.VMEM(padded_rows, jnp.float32),
                    pltpu.VMEM(padded_rows, jnp.float32),
                    pltpu.VMEM((BATCH // 2, 2 * BS, 2 * BS), jnp.bfloat16),
                    pltpu.VMEM((BATCH // 2, 2 * BS, 2 * BS), jnp.bfloat16),
                    pltpu.SMEM((2, sources * (3 * blocks + 2) + 2 * BATCH), jnp.int32),
                ],
            ),
            out_shape=[jax.ShapeDtypeStruct((tokens, width), jnp.bfloat16)]
            + [jax.ShapeDtypeStruct((tokens, width), jnp.bfloat16)] * remote
            + [half_shape] * 4,
            compiler_params=pltpu.CompilerParams(vmem_limit_bytes=48 * 2**20),
            name="gradients",
        )(
            meta,
            table,
            *arrays(q_all + g_all + k_all + v_chunks[c]),
            by_item(norms),
            by_item(dots),
            flat(norms),
            flat(dots),
        )

    def wide(array):
        return array.astype(jnp.float32)

    def reduced(keep, send, first, second):
        got = flip(send, first)
        onward = flip((wide(keep[1]) + wide(got[1])).astype(jnp.bfloat16), second)
        return (wide(keep[0]) + wide(got[0]) + wide(onward)).astype(jnp.bfloat16)

    def to_tokens(array):
        return lax.all_to_all(array, "head", split_axis=0, concat_axis=1, tiled=True)

    dq_parts, dk_parts, dv_parts = [], [], []
    for c in range(len(chunks)):
        outs = gradients(c)
        dq, dq_far = wide(outs[0]), outs[1:sources]
        dk_keep, dk_send, dv_keep, dv_send = outs[sources:]
        for r in range(1, sources):
            dq = dq + wide(shift(dq_far[r - 1], -r))
        dq_parts.append(dq.astype(jnp.bfloat16))
        dk_parts.append(reduced(dk_keep, dk_send, 1, 2))
        dv_parts.append(reduced(dv_keep, dv_send, VALUE_AXES[c], 3 - VALUE_AXES[c]))
    def to_tokens_by_steps(array):
        groups = lax.axis_size("head")
        here = lax.axis_index("head")
        rows = array.reshape(groups, tokens // groups, -1)

        def row(stack, index):
            return lax.dynamic_index_in_dim(stack, lax.rem(index, groups), 0, keepdims=False)

        got = [row(rows, here)]
        for m in range(1, groups):
            pairs = [(i, (i + m) % groups) for i in range(groups)]
            got.append(lax.ppermute(row(rows, here + m), "head", pairs))
        got = jnp.stack(got)
        return jnp.concatenate([row(got, here + groups - j) for j in range(groups)], axis=1)

    dq = to_tokens_by_steps(jnp.concatenate(dq_parts, axis=1))
    dk = to_tokens(jnp.concatenate(dk_parts, axis=1))
    dv = to_tokens(jnp.concatenate(dv_parts, axis=1))
    return dq, dk, dv


def solution(mesh):
    return jax.shard_map(
        on_device,
        mesh=mesh,
        in_specs=(
            P("seq", "head"),
            P("seq", "head"),
            P("seq", "head"),
            P("seq", "head"),
            P("seq", "head"),
            P(None, "head", None),
            P(),
        ),
        out_specs=(P(("seq", "head"), None), P(("seq", "head"), None), P(("seq", "head"), None)),
        check_vma=False,
    )
```

```python
from functools import partial
import math

import jax
import jax.numpy as jnp
from jax import lax
from jax.experimental import pallas as pl
from jax.experimental.pallas import tpu as pltpu
from jax.sharding import PartitionSpec as P

DH = 128
BS = 64
GROUP = 4
BATCH = 16
CUTS = (0.0, 0.5, 1.0)
VALUE_AXES = (1, 2)
JOINED = 4
LOG2E = math.log2(math.e)
SCALE = DH**-0.5
OFF = 1e30
NT = (((1,), (1,)), ((), ()))
TN = (((0,), (0,)), ((), ()))


def dot(a, b, dims=(((1,), (0,)), ((), ()))):
    return lax.dot_general(a, b, dims, preferred_element_type=jnp.float32)


def aligned(start):
    return pl.multiple_of(start, BS)


def place_group(me, key_refs, key_rows, tokens):
    for j, ref in enumerate(key_refs):
        start = aligned(BS + (lax.rem(me, GROUP) ^ j) * tokens)
        key_rows[pl.ds(start, tokens), :] = ref[...]


def zero_ends(key_rows):
    edge = jnp.zeros((BS, DH), key_rows.dtype)
    key_rows[pl.ds(0, BS), :] = edge
    key_rows[pl.ds(key_rows.shape[0] - BS, BS), :] = edge


def local_block(block, group, group_blocks):
    place = block - group * group_blocks
    inside = (place >= 0) & (place < group_blocks)
    return jnp.where(inside, place, 0), inside


def edge_block(src, b, blocks, seq_count, group, group_blocks):
    last = blocks - 1
    if b == 0:
        return local_block(src * blocks - 1, group, group_blocks)
    if b == last:
        return local_block((src + 1) * blocks, group, group_blocks)
    return None


def norm_kernel(sizes, meta, table, *refs):
    seq_count, remote, blocks, heads = sizes
    sources = remote + 1
    tokens = blocks * BS
    q_refs = refs[:sources]
    k_refs = refs[sources : sources + GROUP]
    out_ref, key_rows = refs[sources + GROUP :]
    head = pl.program_id(0)
    me = meta[0]
    group = me // GROUP
    group_blocks = GROUP * blocks
    c2 = SCALE * LOG2E

    @pl.when(head == 0)
    def _():
        zero_ends(key_rows)

    place_group(me, k_refs, key_rows, tokens)
    globs = [local_block(meta[1 + j], group, group_blocks) for j in range(2)]
    glob_keys = [key_rows[pl.ds(aligned(BS + p * BS), BS), :] for p, _ in globs]

    pos = lax.rem(me, GROUP)
    lane = lax.broadcasted_iota(jnp.int32, (1, 2 * BS), 1)
    for r in range(sources):
        src = lax.rem(me - GROUP * r + seq_count, seq_count)
        for t in range(blocks // 2):
            q = q_refs[r][pl.ds(t * 2 * BS, 2 * BS), :]
            tiles, off = [], []
            if r == 0:
                start = aligned((pos * blocks + 2 * t) * BS)
                tiles.append(key_rows[pl.ds(start, 4 * BS), :])
                first = jnp.where(pos > 0, 0.0, OFF) if t == 0 else 0.0
                last = jnp.where(pos < GROUP - 1, 0.0, OFF) if t == blocks // 2 - 1 else 0.0
                off += [(first, OFF), None, None, (OFF, last)]
            for j in range(2):
                tiles.append(glob_keys[j])
                here = jnp.where(globs[j][1], 0.0, OFF)
                off.append((here, here))
            for u in range(2):
                b = 2 * t + u
                found = [
                    local_block(table[((src * blocks + b) * heads + head) * 3 + j], group, group_blocks)
                    for j in range(3)
                ]
                edge = edge_block(src, b, blocks, seq_count, group, group_blocks)
                if r > 0 and edge is not None:
                    found.append(edge)
                for place, inside in found:
                    tiles.append(key_rows[pl.ds(aligned(BS + place * BS), BS), :])
                    here = jnp.where(inside, 0.0, OFF)
                    off.append((here, OFF) if u == 0 else (OFF, here))
            products = dot(jnp.concatenate(tiles, axis=0), q, NT)
            scores = []
            for j, pair in enumerate(off):
                s = products[j * BS : (j + 1) * BS] * c2
                if pair is not None:
                    s = s - jnp.where(lane < BS, pair[0], pair[1])
                scores.append(s)
            top = scores[0]
            for s in scores[1:]:
                top = jnp.maximum(top, s)
            top = jnp.max(top, axis=0, keepdims=True)
            total = jnp.exp2(scores[0] - top)
            for s in scores[1:]:
                total = total + jnp.exp2(s - top)
            found = top + jnp.log2(jnp.sum(total, axis=0, keepdims=True))
            out_ref[r, 0, pl.ds(2 * t, 1), :] = found[:, :BS]
            out_ref[r, 0, pl.ds(2 * t + 1, 1), :] = found[:, BS:]


def grads_kernel(sizes, value_axis, head0, meta, table, *refs):
    seq_count, remote, blocks, heads = sizes
    sources = remote + 1
    tokens = blocks * BS
    refs = list(refs)

    def take(count):
        taken = refs[:count]
        del refs[:count]
        return taken

    q_refs, g_refs = take(sources), take(sources)
    k_refs, v_refs = take(GROUP), take(GROUP)
    norm_ref, dot_ref, norm_flat, dot_flat = take(4)
    (dq_own,) = take(1)
    dq_far = take(remote)
    dk_keep, dk_send, dv_keep, dv_send = take(4)
    q_rows, g_rows, k_rows, v_rows, dq_sum, dk_sum, dv_sum, w_kept, ds_kept, listed = refs
    head = pl.program_id(0) + head0
    me = meta[0]
    pos = lax.rem(me, GROUP)
    group = me // GROUP
    group_blocks = GROUP * blocks
    c2 = SCALE * LOG2E

    @pl.when(pl.program_id(0) == 0)
    def _():
        zero_ends(k_rows)
        zero_ends(v_rows)

    place_group(me, k_refs, k_rows, tokens)
    place_group(me, v_refs, v_rows, tokens)
    for r in range(sources):
        q_rows[pl.ds(r * tokens, tokens), :] = q_refs[r][...]
        g_rows[pl.ds(r * tokens, tokens), :] = g_refs[r][...]
    dk_sum[...] = jnp.zeros_like(dk_sum)
    dv_sum[...] = jnp.zeros_like(dv_sum)
    dq_sum[...] = jnp.zeros_like(dq_sum)

    count = jnp.int32(0)

    def note(count, item, place, inside):
        listed[0, count] = item
        listed[1, count] = place
        return count + inside.astype(jnp.int32)

    for r in range(sources):
        src = lax.rem(me - GROUP * r + seq_count, seq_count)
        for b in range(blocks):
            item = r * blocks + b
            for j in range(3):
                entry = table[((src * blocks + b) * heads + head) * 3 + j]
                count = note(count, item, *local_block(entry, group, group_blocks))
            if r > 0:
                found = edge_block(src, b, blocks, seq_count, group, group_blocks)
                if found is not None:
                    count = note(count, item, *found)
    for u in range(2 * BATCH):
        listed[0, count + u] = 0
        listed[1, count + u] = 0

    lane = lax.broadcasted_iota(jnp.int32, (1, 2 * BS), 1)

    globs = [local_block(meta[1 + j], group, group_blocks) for j in range(2)]
    wide = tokens

    spans = [pl.ds(aligned(BS + p * BS), BS) for p, _ in globs]
    k = jnp.concatenate([k_rows[s, :] for s in spans], axis=0)
    v = jnp.concatenate([v_rows[s, :] for s in spans], axis=0)
    off = [jnp.where(inside, 0.0, OFF) for _, inside in globs]
    dk = jnp.zeros((2 * BS, DH), jnp.float32)
    dv = jnp.zeros((2 * BS, DH), jnp.float32)
    for r in range(sources):
        for t in range(tokens // wide):
            rows = pl.ds(r * tokens + t * wide, wide)
            q, g = q_rows[rows, :], g_rows[rows, :]
            norm = norm_flat[r, 0, :, t * wide : (t + 1) * wide]
            rdot = dot_flat[r, 0, :, t * wide : (t + 1) * wide]
            s = dot(k, q, NT) * c2
            w = jnp.concatenate(
                [jnp.exp2(s[:BS] - (norm + off[0])), jnp.exp2(s[BS:] - (norm + off[1]))],
                axis=0,
            )
            ds = w * (dot(v, g, NT) - rdot)
            wb, dsb = w.astype(jnp.bfloat16), ds.astype(jnp.bfloat16)
            dq_sum[rows, :] += dot(dsb, k, TN)
            dk = dk + dot(dsb, q)
            dv = dv + dot(wb, g)
    for j, span in enumerate(spans):
        dk_sum[span, :] += dk[j * BS : (j + 1) * BS]
        dv_sum[span, :] += dv[j * BS : (j + 1) * BS]

    def places(step):
        rows, spans = [], []
        for u in range(BATCH):
            rows.append(pl.ds(aligned(listed[0, step * BATCH + u] * BS), BS))
            spans.append(pl.ds(aligned(BS + listed[1, step * BATCH + u] * BS), BS))
        return rows, spans

    def joined(ref, slices):
        return jnp.concatenate([ref[x, :] for x in slices], axis=0)

    def weigh(step):
        rows, spans = places(step)
        weighed = []
        for first in range(0, BATCH, JOINED):
            these = slice(first, first + JOINED)
            s = dot(joined(k_rows, spans[these]), joined(q_rows, rows[these]), NT)
            dw = dot(joined(v_rows, spans[these]), joined(g_rows, rows[these]), NT)
            for t in range(JOINED // 2):
                norms, dots = [], []
                for u in (first + 2 * t, first + 2 * t + 1):
                    item = listed[0, step * BATCH + u]
                    off = jnp.where(step * BATCH + u < count, 0.0, OFF)
                    norms.append(norm_ref[0, pl.ds(item, 1), :] + off)
                    dots.append(dot_ref[0, pl.ds(item, 1), :])
                part = slice(t * 2 * BS, (t + 1) * 2 * BS)
                both = s[part, part] * c2
                w = jnp.concatenate(
                    [
                        jnp.exp2(both[:BS] - jnp.where(lane < BS, norms[0], OFF)),
                        jnp.exp2(both[BS:] - jnp.where(lane < BS, OFF, norms[1])),
                    ],
                    axis=0,
                )
                ds = w * (dw[part, part] - jnp.where(lane < BS, dots[0], dots[1]))
                weighed.append((w.astype(jnp.bfloat16), ds.astype(jnp.bfloat16)))
        return weighed

    def keep_weighed(weighed):
        for t, (w, ds) in enumerate(weighed):
            w_kept[t], ds_kept[t] = w, ds

    def batch(step, carry):
        held = [(w_kept[t], ds_kept[t]) for t in range(BATCH // 2)]
        following = weigh(step + 1)
        rows, spans = places(step)
        done = []
        for t, (wb, dsb) in enumerate(held):
            pair = slice(2 * t, 2 * t + 2)
            q, g, k = joined(q_rows, rows[pair]), joined(g_rows, rows[pair]), joined(k_rows, spans[pair])
            done.append((dot(dsb, k, TN), dot(dsb, q), dot(wb, g)))
        keep_weighed(following)
        for u in range(BATCH):
            dq, dk, dv = done[u // 2]
            part = slice((u % 2) * BS, (u % 2 + 1) * BS)
            dq_sum[rows[u], :] += dq[part]
            dk_sum[spans[u], :] += dk[part]
            dv_sum[spans[u], :] += dv[part]
        return carry

    keep_weighed(weigh(0))
    pairs = blocks // 2
    for t in range(pairs):
        rows = pl.ds(t * 2 * BS, 2 * BS)
        q, g = q_refs[0][rows, :], g_refs[0][rows, :]
        start = aligned((pos * blocks + 2 * t) * BS)
        span = pl.ds(start, 4 * BS)
        k, v = k_rows[span, :], v_rows[span, :]
        norm = norm_flat[0, 0, :, t * 2 * BS : (t + 1) * 2 * BS]
        rdot = dot_flat[0, 0, :, t * 2 * BS : (t + 1) * 2 * BS]
        first = jnp.where(lane < BS, norm, OFF)
        last = jnp.where(lane < BS, OFF, norm)
        if t == 0:
            first = first + jnp.where(pos > 0, 0.0, OFF)
        if t == pairs - 1:
            last = last + jnp.where(pos < GROUP - 1, 0.0, OFF)
        s = dot(k, q, NT) * c2
        w = jnp.concatenate(
            [
                jnp.exp2(s[:BS] - first),
                jnp.exp2(s[BS : 3 * BS] - norm),
                jnp.exp2(s[3 * BS :] - last),
            ],
            axis=0,
        )
        ds = w * (dot(v, g, NT) - rdot)
        wb, dsb = w.astype(jnp.bfloat16), ds.astype(jnp.bfloat16)
        dq_sum[rows, :] += dot(dsb, k, TN)
        dk_sum[span, :] += dot(dsb, q)
        dv_sum[span, :] += dot(wb, g)

    lax.fori_loop(0, (count + BATCH - 1) // BATCH, batch, 0)

    dq_own[...] = (dq_sum[pl.ds(0, tokens), :] * SCALE).astype(jnp.bfloat16)
    for r in range(remote):
        dq_far[r][...] = (dq_sum[pl.ds((r + 1) * tokens, tokens), :] * SCALE).astype(jnp.bfloat16)
    for j in range(GROUP):
        rows = pl.ds(aligned(BS + (pos ^ j) * tokens), tokens)
        for total, keep, send, axis, factor in (
            (dk_sum, dk_keep, dk_send, 1, SCALE),
            (dv_sum, dv_keep, dv_send, value_axis, 1.0),
        ):
            slot = (j >> 1) if axis == 1 else (j & 1)
            target = send if j & axis else keep
            part = total[rows, :]
            part = part * factor if factor != 1.0 else part
            target[slot] = part.astype(jnp.bfloat16)


def on_device(
    queries, key_states, value_states, forward_out, grad_out, random_blocks, global_blocks
):
    seq_count = lax.axis_size("seq")
    me = lax.axis_index("seq")
    tokens = queries.shape[0]
    blocks = tokens // BS
    heads = queries.shape[1] // DH
    sources = seq_count // GROUP
    remote = sources - 1
    sizes = (seq_count, remote, blocks, heads)

    def shift(array, r):
        pairs = [(i, (i + GROUP * r) % seq_count) for i in range(seq_count)]
        return lax.ppermute(array, "seq", pairs)

    def flip(array, j):
        return lax.ppermute(array, "seq", [(i, i ^ j) for i in range(seq_count)])

    def after(array, other):
        return lax.optimization_barrier((array, other))[0]

    def whole(array, place=None):
        return [(array, place, 0)]

    cuts = [round(heads * x) for x in CUTS]
    chunks = list(zip(cuts[:-1], cuts[1:]))
    k_z = flip(key_states, 2)
    q_all = whole(queries)
    for r in range(1, sources):
        q_all += whole(shift(queries, r))
    kv_x = flip(jnp.stack([key_states, value_states]), 1)
    k_all = whole(key_states) + whole(kv_x, 0) + whole(k_z) + whole(flip(k_z, 1))

    v_chunks, previous = [], k_z
    g_all = whole(grad_out)
    for r in range(1, sources):
        g_all += whole(shift(grad_out, r))
    for c, (low, high) in enumerate(chunks):
        cut = slice(low * DH, high * DH)
        v = after(value_states[:, cut], previous)
        own = [(value_states, None, low), (kv_x, 1, low)]
        if c == 0:
            v_z = flip(v, 2)
            v_all = own + [(v_z, None, 0), (flip(v_z, 1), None, 0)]
            previous = v_z
        else:
            v_z = flip(jnp.stack([v, kv_x[1][:, cut]]), 2)
            v_all = own + [(v_z, 0, 0), (v_z, 1, 0)]
            previous = v_z
        v_chunks.append(v_all)

    meta = jnp.concatenate([me.astype(jnp.int32)[None], global_blocks.astype(jnp.int32)])
    table = random_blocks.reshape(-1)

    def spec(operand, head0):
        _, place, first = operand
        if place is None:
            return pl.BlockSpec((tokens, DH), lambda h, *_: (0, h + head0 + first))
        return pl.BlockSpec((None, tokens, DH), lambda h, *_: (place, 0, h + head0 + first))

    def arrays(operands):
        return [array for array, _, _ in operands]

    padded_rows = (GROUP * tokens + 2 * BS, DH)
    partial_norms = pl.pallas_call(
        partial(norm_kernel, sizes),
        grid_spec=pltpu.PrefetchScalarGridSpec(
            num_scalar_prefetch=2,
            grid=(heads,),
            in_specs=[spec(x, 0) for x in q_all + k_all],
            out_specs=pl.BlockSpec((sources, 1, blocks, BS), lambda h, *_: (0, h, 0, 0)),
            scratch_shapes=[pltpu.VMEM(padded_rows, jnp.bfloat16)],
        ),
        out_shape=jax.ShapeDtypeStruct((sources, heads, blocks, BS), jnp.float32),
        compiler_params=pltpu.CompilerParams(vmem_limit_bytes=48 * 2**20),
        name="partial_norms",
    )(meta, table, *arrays(q_all + k_all))

    row_dot = jnp.sum(
        grad_out.astype(jnp.float32).reshape(tokens, heads, DH)
        * forward_out.astype(jnp.float32).reshape(tokens, heads, DH),
        axis=-1,
    )
    row_dot = row_dot.reshape(blocks, BS, heads).transpose(2, 0, 1)

    mine = jnp.concatenate([partial_norms, row_dot[None]], axis=0)
    told = [mine] + [shift(mine, r) for r in range(1, sources)]
    norms, dots = [], []
    for r in range(sources):
        parts = jnp.stack([told[k][(r - k) % sources] for k in range(sources)])
        top = jnp.max(parts, axis=0)
        norms.append(top + jnp.log2(jnp.sum(jnp.exp2(parts - top), axis=0)))
        dots.append(told[r][sources])
    norms, dots = jnp.stack(norms), jnp.stack(dots)

    def by_item(array):
        array = array.transpose(1, 0, 2, 3).reshape(heads, sources * blocks, BS)
        return jnp.concatenate([array, array], axis=-1)

    def flat(array):
        return array.reshape(sources, heads, 1, tokens)

    def gradients(c):
        head0, count = chunks[c][0], chunks[c][1] - chunks[c][0]
        width = count * DH
        item_spec = pl.BlockSpec((1, sources * blocks, 2 * BS), lambda h, *_: (h + head0, 0, 0))
        flat_spec = pl.BlockSpec((sources, 1, 1, tokens), lambda h, *_: (0, h + head0, 0, 0))
        out_column = pl.BlockSpec((tokens, DH), lambda h, *_: (0, h))
        half_spec = pl.BlockSpec((GROUP // 2, tokens, DH), lambda h, *_: (0, 0, h))
        half_shape = jax.ShapeDtypeStruct((GROUP // 2, tokens, width), jnp.bfloat16)
        return pl.pallas_call(
            partial(grads_kernel, sizes, VALUE_AXES[c], head0),
            grid_spec=pltpu.PrefetchScalarGridSpec(
                num_scalar_prefetch=2,
                grid=(count,),
                in_specs=[spec(x, head0) for x in q_all]
                + [spec(x, head0) for x in g_all]
                + [spec(x, head0) for x in k_all]
                + [spec(x, 0) for x in v_chunks[c]]
                + [item_spec] * 2
                + [flat_spec] * 2,
                out_specs=[out_column] * sources + [half_spec] * 4,
                scratch_shapes=[
                    pltpu.VMEM((sources * tokens, DH), jnp.bfloat16),
                    pltpu.VMEM((sources * tokens, DH), jnp.bfloat16),
                    pltpu.VMEM(padded_rows, jnp.bfloat16),
                    pltpu.VMEM(padded_rows, jnp.bfloat16),
                    pltpu.VMEM((sources * tokens, DH), jnp.float32),
                    pltpu.VMEM(padded_rows, jnp.float32),
                    pltpu.VMEM(padded_rows, jnp.float32),
                    pltpu.VMEM((BATCH // 2, 2 * BS, 2 * BS), jnp.bfloat16),
                    pltpu.VMEM((BATCH // 2, 2 * BS, 2 * BS), jnp.bfloat16),
                    pltpu.SMEM((2, sources * (3 * blocks + 2) + 2 * BATCH), jnp.int32),
                ],
            ),
            out_shape=[jax.ShapeDtypeStruct((tokens, width), jnp.bfloat16)]
            + [jax.ShapeDtypeStruct((tokens, width), jnp.bfloat16)] * remote
            + [half_shape] * 4,
            compiler_params=pltpu.CompilerParams(vmem_limit_bytes=48 * 2**20),
            name="gradients",
        )(
            meta,
            table,
            *arrays(q_all + g_all + k_all + v_chunks[c]),
            by_item(norms),
            by_item(dots),
            flat(norms),
            flat(dots),
        )

    def wide(array):
        return array.astype(jnp.float32)

    def reduced(keep, send, first, second):
        got = flip(send, first)
        onward = flip((wide(keep[1]) + wide(got[1])).astype(jnp.bfloat16), second)
        return (wide(keep[0]) + wide(got[0]) + wide(onward)).astype(jnp.bfloat16)

    def to_tokens(array):
        return lax.all_to_all(array, "head", split_axis=0, concat_axis=1, tiled=True)

    dq_parts, dk_parts, dv_parts = [], [], []
    for c in range(len(chunks)):
        outs = gradients(c)
        dq, dq_far = wide(outs[0]), outs[1:sources]
        dk_keep, dk_send, dv_keep, dv_send = outs[sources:]
        for r in range(1, sources):
            dq = dq + wide(shift(dq_far[r - 1], -r))
        dq_parts.append(dq.astype(jnp.bfloat16))
        dk_parts.append(reduced(dk_keep, dk_send, 1, 2))
        dv_parts.append(reduced(dv_keep, dv_send, VALUE_AXES[c], 3 - VALUE_AXES[c]))
    def to_tokens_by_steps(array):
        groups = lax.axis_size("head")
        here = lax.axis_index("head")
        rows = array.reshape(groups, tokens // groups, -1)

        def row(stack, index):
            return lax.dynamic_index_in_dim(stack, lax.rem(index, groups), 0, keepdims=False)

        got = [row(rows, here)]
        for m in range(1, groups):
            pairs = [(i, (i + m) % groups) for i in range(groups)]
            got.append(lax.ppermute(row(rows, here + m), "head", pairs))
        got = jnp.stack(got)
        return jnp.concatenate([row(got, here + groups - j) for j in range(groups)], axis=1)

    dq = to_tokens_by_steps(jnp.concatenate(dq_parts, axis=1))
    dk = to_tokens(jnp.concatenate(dk_parts, axis=1))
    dv = to_tokens(jnp.concatenate(dv_parts, axis=1))
    return dq, dk, dv


def solution(mesh):
    return jax.shard_map(
        on_device,
        mesh=mesh,
        in_specs=(
            P("seq", "head"),
            P("seq", "head"),
            P("seq", "head"),
            P("seq", "head"),
            P("seq", "head"),
            P(None, "head", None),
            P(),
        ),
        out_specs=(P(("seq", "head"), None), P(("seq", "head"), None), P(("seq", "head"), None)),
        check_vma=False,
    )
```
